256 devices in a mesh: section: 16 (over y_lo, z), ctx: 16 (over y_hi, x, core).
Axes of the slice: x: 4, y: 4 (y_hi: 2, y_lo: 2; y = y_hi * 2 + y_lo), z: 8, core: 2. Of those that a mesh axis runs over, the one named last changes fastest.
Arguments:
- layer_input: bfloat16 [16, 4096, 2048], P('section', 'ctx'), may hold values from -6 to 6
- qk_weight: bfloat16 [16, 2048, 2048], P('section'), may hold values from -0.125 to 0.125
- norm_gain: float32 [16, 2048], P('section'), may hold values from 0.25 to 1.75
- out_gain: float32 [16, 128], P('section'), may hold values from 0.25 to 1.75
- log_decay: float32 [16, 16, 4096], P('section', None, 'ctx'), may hold values from -1 to 0
- write_rate: float32 [16, 16, 4096], P('section', None, 'ctx'), may hold values from 0 to 1
Outputs:
- layer_output: bfloat16 [16, 4096, 2048], P('section', 'ctx')
The draws below stay inside these ranges and needn't reach their ends.
All inputs are finite; a program needn't handle non-finite values.
Results may differ from the reference program's by a relative error of at most 0.015.
Values may be sent and summed in bfloat16 or wider, within the bound.
No kernel may reach another device: no remote copies, remote signals or barrier semaphores. Data moves between devices by JAX's collectives and lax.ppermute only.
A program may use at most 192 MiB of HBM per device.

```python
import math
import jax
import jax.numpy as jnp
from jax import lax

D = 2048
DK = 128
VALUE_HEADS = 16
CH = 64
TOK_DEV = 256
SEQUENCE_TOKENS = 4096
N_SECTION = 16


def slow_heads(key, slow_share):
    head_key = jax.random.fold_in(key, 101)
    return jax.random.uniform(head_key, (N_SECTION, VALUE_HEADS, 1)) < slow_share


def draw_log_decay(key, part):
    slow_share = 0.5
    slow_mask = slow_heads(key, slow_share)
    key = jax.random.fold_in(key, 1)
    jitter_random_key, partition_random_key, spike_random_key, extent_random_key = jax.random.split(key, 4)
    jitter_level = jnp.exp(jax.random.uniform(jitter_random_key, (N_SECTION, VALUE_HEADS, SEQUENCE_TOKENS), minval=math.log(0.6), maxval=math.log(1.6)))
    partition_factor = jnp.exp(jax.random.uniform(partition_random_key, (N_SECTION, VALUE_HEADS, SEQUENCE_TOKENS // TOK_DEV, 1), minval=math.log(0.5), maxval=math.log(2.0)))
    partition_factor = jnp.broadcast_to(partition_factor, (N_SECTION, VALUE_HEADS, SEQUENCE_TOKENS // TOK_DEV, TOK_DEV)).reshape(N_SECTION, VALUE_HEADS, SEQUENCE_TOKENS)
    spike_mask = jax.random.uniform(spike_random_key, (N_SECTION, 1, SEQUENCE_TOKENS)) < 2.0 / SEQUENCE_TOKENS
    spike_extent = jax.random.uniform(extent_random_key, (N_SECTION, VALUE_HEADS, SEQUENCE_TOKENS), minval=0.22, maxval=0.69)
    gradual_decay_rate = -(0.2 / SEQUENCE_TOKENS) * jitter_level * partition_factor - jnp.where(spike_mask, spike_extent, 0.0)
    fast_rate = -jitter_level / 40.0
    return jnp.where(slow_mask, gradual_decay_rate, fast_rate).astype(jnp.float32)


def draw_write_rate(key, part):
    slow_share = 0.5
    slow_mask = slow_heads(key, slow_share)
    key = jax.random.fold_in(key, 2)
    key_slow, key_fast = jax.random.split(key, 2)
    gradual_decay_rate = 0.8 * DK / SEQUENCE_TOKENS * jnp.exp(jax.random.uniform(key_slow, (N_SECTION, VALUE_HEADS, SEQUENCE_TOKENS), minval=math.log(0.5), maxval=math.log(2.0)))
    fast_rate = jax.random.uniform(key_fast, (N_SECTION, VALUE_HEADS, SEQUENCE_TOKENS), minval=0.2, maxval=0.9)
    return jnp.where(slow_mask, gradual_decay_rate, fast_rate).astype(jnp.float32)


def steps_of(stream_key, extent, cuts, smallest, high):
    level = 1.0
    for dim, blocks in cuts:
        steps = jax.random.uniform(jax.random.fold_in(jax.random.fold_in(stream_key, 6), dim), (blocks,), jnp.float32, smallest / len(cuts), high / len(cuts))
        level = level * jnp.repeat(jnp.exp(steps), extent[dim] // blocks).reshape((-1,) + (1,) * (len(extent) - 1 - dim))
    return level


def noise(rng, dims, scale, bound, cuts=(), kind=jnp.bfloat16):
    level = steps_of(rng, dims, cuts, -0.22, 0.18) if cuts else 1.0
    values = jax.random.normal(rng, dims, jnp.float32) * scale * level
    return jnp.minimum(jnp.maximum(values, -bound), bound).astype(kind)


def setup_inputs(seed: int = 0) -> dict:
    keys = jax.random.split(jax.random.key(seed), 7)
    layer_input = noise(keys[0], (N_SECTION, SEQUENCE_TOKENS, D), 1.0, 6.0, ((0, 16), (1, 16)))
    qk_weight = noise(keys[1], (N_SECTION, D, D), D ** -0.5, 0.125, ((0, 16),))
    norm_gain = jnp.clip(1.0 + 0.15 * jax.random.normal(keys[2], (N_SECTION, D), jnp.float32), 0.25, 1.75)
    out_gain = jnp.clip(1.0 + 0.15 * jax.random.normal(keys[3], (N_SECTION, DK), jnp.float32), 0.25, 1.75)
    log_decay = draw_log_decay(jax.random.fold_in(keys[6], 71), 0)
    write_rate = draw_write_rate(jax.random.fold_in(keys[6], 71), 0)
    return {"layer_input": layer_input, "qk_weight": qk_weight, "norm_gain": norm_gain, "out_gain": out_gain, "log_decay": log_decay, "write_rate": write_rate}


def rounded(array):
    return lax.optimization_barrier(array.astype(jnp.bfloat16)).astype(jnp.float32)

def unit_inverse(coupling, block_size):
    highest = lax.Precision.HIGHEST
    eye_block = jnp.eye(block_size, dtype=jnp.float32)
    power = -coupling
    inverse = eye_block + power
    span = 2
    while span < block_size:
        power = jnp.einsum('nhij,nhjk->nhik', power, power, precision=highest)
        inverse = inverse + jnp.einsum('nhij,nhjk->nhik', inverse, power, precision=highest)
        span = span * 2
    return inverse

def group_terms(queries, key_vectors, values, log_rates, rates, block_size):
    tokens, head_count, head_size = queries.shape
    block_count = tokens // block_size
    highest = lax.Precision.HIGHEST

    def blocks(array):
        return array.astype(jnp.float32).reshape(block_count, block_size, head_count, head_size).transpose(0, 2, 1, 3)
    query_blocks = blocks(queries)
    key_blocks = blocks(key_vectors)
    value_blocks = blocks(values)
    log_blocks = log_rates.reshape(head_count, block_count, block_size).transpose(1, 0, 2)
    rate_blocks = rates.reshape(head_count, block_count, block_size).transpose(1, 0, 2)
    cumul = jnp.cumsum(log_blocks, axis=2)
    block_ends = cumul[:, :, -1:]
    row_index = lax.broadcasted_iota(jnp.int32, (block_size, block_size), 0)
    col_index = lax.broadcasted_iota(jnp.int32, (block_size, block_size), 1)
    lower_incl = col_index <= row_index
    strict = col_index < row_index
    log_gaps = cumul[:, :, :, None] - cumul[:, :, None, :]
    decays = jnp.exp(jnp.where(lower_incl, log_gaps, -jnp.inf))
    key_gram = jnp.einsum('nhid,nhjd->nhij', key_blocks, key_blocks, precision=highest)
    coupling = jnp.where(strict, rate_blocks[..., None] * decays * key_gram, 0.0)
    inverse = rounded(unit_inverse(coupling, block_size))
    right_side = rounded(jnp.concatenate([rate_blocks[..., None] * value_blocks, (rate_blocks * jnp.exp(cumul))[..., None] * key_blocks], axis=3))
    solved = rounded(jnp.einsum('nhij,nhjd->nhid', inverse, right_side, precision=highest))
    solved_values = solved[..., :head_size]
    solved_keys = solved[..., head_size:]
    carried = rounded(key_blocks * jnp.exp(block_ends - cumul)[..., None])
    transition = jnp.exp(block_ends)[..., None] * jnp.eye(head_size, dtype=jnp.float32) - jnp.einsum('nhid,nhie->nhde', carried, solved_keys, precision=highest)
    block_state = jnp.einsum('nhid,nhie->nhde', carried, solved_values, precision=highest)
    scores = rounded(decays * jnp.einsum('nhid,nhjd->nhij', query_blocks, key_blocks, precision=highest))
    query_reads = rounded(jnp.exp(cumul)[..., None] * query_blocks - jnp.einsum('nhij,nhjd->nhid', scores, solved_keys, precision=highest))
    local_part = jnp.einsum('nhij,nhjd->nhid', scores, solved_values, precision=highest)
    return (query_reads, local_part, transition, block_state)

def run_blocks(query_reads, local_part, transition, block_state, start_state):
    highest = lax.Precision.HIGHEST

    def advance_block(current, pieces):
        read_part, local_term, step_trans, step_state = pieces
        emitted = jnp.einsum('hid,hde->hie', read_part, rounded(current), precision=highest) + local_term
        advanced = jnp.einsum('hde,hef->hdf', step_trans, current, precision=highest) + step_state
        return (advanced, emitted)
    final_state, emitted_all = lax.scan(advance_block, start_state, (query_reads, local_part, transition, block_state))
    block_count, head_count, block_size, head_size = emitted_all.shape
    return emitted_all.transpose(0, 2, 1, 3).reshape(block_count * block_size, head_count, head_size)

def project(rows_in, weight, gain_in, head_count, head_size):
    rows_float = rows_in.astype(jnp.float32)
    normed = (rows_float * lax.rsqrt(lax.optimization_barrier(jnp.mean(rows_float * rows_float, axis=-1, keepdims=True)) + 1e-06) * gain_in).astype(jnp.bfloat16)
    projected = jnp.dot(normed, weight, preferred_element_type=jnp.float32)
    tokens = rows_in.shape[0]
    key_heads = head_count // 2
    queries = projected[:, :key_heads * head_size].reshape(tokens, key_heads, head_size).astype(jnp.bfloat16)
    raw_keys = projected[:, key_heads * head_size:].reshape(tokens, key_heads, head_size)
    unit_keys = (raw_keys * lax.rsqrt(lax.optimization_barrier(jnp.sum(raw_keys * raw_keys, axis=-1, keepdims=True)) + 1e-06)).astype(jnp.bfloat16)
    queries = jnp.repeat(queries, 2, axis=1)
    unit_keys = jnp.repeat(unit_keys, 2, axis=1)
    values = normed.reshape(tokens, head_count, head_size)
    return (queries, unit_keys, values)

def finish(rows_in, mixed, gain_out):
    scaled = mixed * lax.rsqrt(lax.optimization_barrier(jnp.mean(mixed * mixed, axis=-1, keepdims=True)) + 1e-06) * gain_out
    branch = scaled.reshape(rows_in.shape[0], -1).astype(jnp.bfloat16)
    branch = lax.optimization_barrier(branch)
    return (rows_in.astype(jnp.float32) + branch.astype(jnp.float32)).astype(jnp.bfloat16)

def one_layer(operands):
    rows_in, weight, gain_in, gain_out, log_rates, rates = operands
    head_count = log_rates.shape[0]
    head_size = gain_out.shape[0]
    queries, unit_keys, values = project(rows_in, weight, gain_in, head_count, head_size)
    query_reads, local_part, transition, block_state = group_terms(queries, unit_keys, values, log_rates, rates, CH)
    start_state = jnp.zeros((head_count, head_size, head_size), jnp.float32)
    mixed = run_blocks(query_reads, local_part, transition, block_state, start_state)
    return finish(rows_in, mixed, gain_out)

def reference(layer_input, qk_weight, norm_gain, out_gain, log_decay, write_rate):
    results = lax.map(one_layer, (layer_input, qk_weight, norm_gain, out_gain, log_decay, write_rate))
    return jnp.roll(results, 1, axis=0)
```

```python
import jax
import jax.numpy as jnp
from jax import lax
from jax.experimental import pallas as pl
from jax.experimental.pallas import tpu as pltpu
from jax.sharding import PartitionSpec as P

F32 = jnp.float32
BF16 = jnp.bfloat16
EPS = 1e-6
HALF = 128
BASE = 16
GROUP = 4


def mm(a, b):
    return jnp.dot(a, b, preferred_element_type=F32)


def iota(shape, dim):
    return lax.broadcasted_iota(jnp.int32, shape, dim)


def base_inverses(couplings):
    lanes = HALF
    count = len(couplings)
    blocks = lanes // BASE
    lane = iota((BASE, lanes), 1)
    packed = []
    for c in couplings:
        d = jnp.zeros((BASE, lanes), F32)
        for blk in range(blocks):
            d = jnp.where(lane // BASE == blk, c[blk * BASE : (blk + 1) * BASE, :], d)
        packed.append(d)
    d = jnp.concatenate(packed, axis=0)
    rows = count * BASE
    lane_all = iota((rows, lanes), 1)
    x = jnp.where(iota((rows, lanes), 0) % BASE == lane_all % BASE, 1.0, 0.0).astype(F32)
    x = x.reshape(count, BASE, lanes)
    for j in range(BASE - 1):
        spread = jnp.take_along_axis(d, lane_all // BASE * BASE + j, axis=1)
        x = x - spread.reshape(count, BASE, lanes) * x[:, j : j + 1, :]
    full = []
    for n in range(count):
        full.append(
            jnp.concatenate(
                [jnp.where(lane // BASE == blk, x[n], 0.0) for blk in range(blocks)], axis=0
            ).astype(BF16)
        )
    return full


def merge(x, coupling, m):
    size = x.shape[0]
    pairs = size // (2 * m)
    lane = iota((m, size), 1)
    left, odd = [], []
    for p in range(pairs):
        at = (2 * p + 1) * m
        left.append(jnp.where(lane // m == 2 * p, coupling[at : at + m, :], jnp.zeros((), BF16)))
        odd.append(x[at : at + m, :])
    y = mm(jnp.concatenate(left, axis=0), x).astype(BF16)
    spread = []
    for p in range(pairs):
        spread += [jnp.zeros((m, size), BF16), y[p * m : (p + 1) * m, :]]
    z = mm(jnp.concatenate(odd, axis=0), jnp.concatenate(spread, axis=0)).astype(BF16)
    out = []
    for p in range(pairs):
        out += [x[2 * p * m : (2 * p + 1) * m, :], odd[p] - z[p * m : (p + 1) * m, :]]
    return jnp.concatenate(out, axis=0)


def local_kernel(
    x_ref, gain_ref, decay_ref, rate_ref, wq_ref, wk_ref, ts_ref, qr_ref, loc_ref, normed, rows, cols
):
    step = pl.program_id(0)
    tokens = x_ref.shape[0]
    half = HALF

    @pl.when(step == 0)
    def _():
        xf = x_ref[...].astype(F32)
        normed[...] = (
            xf * lax.rsqrt(jnp.mean(xf * xf, axis=-1, keepdims=True) + EPS) * gain_ref[...]
        ).astype(BF16)
        upto = (iota((tokens, tokens), 0) <= iota((tokens, tokens), 1)).astype(BF16)
        logs = decay_ref[...]
        hi = logs.astype(BF16)
        rest = logs - hi.astype(F32)
        mid = rest.astype(BF16)
        low = (rest - mid.astype(F32)).astype(BF16)
        cumul = mm(hi, upto) + (mm(mid, upto) + mm(low, upto))
        rates = rate_ref[...]
        for s in range(rows.shape[0]):
            both = jnp.concatenate(
                [cumul[s * GROUP : (s + 1) * GROUP], rates[s * GROUP : (s + 1) * GROUP]], axis=0
            )
            rows[s] = both
            cols[s] = both.T

    pq = mm(normed[...], wq_ref[...])
    pk = mm(normed[...], wk_ref[...])
    row_all = rows[step]
    col_all = cols[step]
    ri = iota((half, half), 0)
    ci = iota((half, half), 1)
    incl = ci <= ri
    strict = ci < ri

    heads = []
    for h in range(GROUP):
        kh = h // 2
        at = kh * 128
        if h % 2 == 0:
            q = pq[:, at : at + 128].astype(BF16)
            raw = pk[:, at : at + 128]
            k = (raw * lax.rsqrt(jnp.sum(raw * raw, axis=-1, keepdims=True) + EPS)).astype(BF16)
            kt = k.T
            kk = mm(k, kt)
            qk = mm(q, kt)
            kf = k.astype(F32)
            qf = q.astype(F32)
            ktf = kt.astype(F32)
        c_col = col_all[:, h : h + 1]
        c_row = row_all[h : h + 1, :]
        b_col = col_all[:, GROUP + h : GROUP + h + 1]
        c_end = c_row[:, tokens - 1 : tokens]
        d00 = jnp.where(incl, jnp.exp(jnp.minimum(c_col[:half] - c_row[:, :half], 0.0)), 0.0)
        d11 = jnp.where(incl, jnp.exp(jnp.minimum(c_col[half:] - c_row[:, half:], 0.0)), 0.0)
        d10 = jnp.exp(c_col[half:] - c_row[:, :half])
        l00 = jnp.where(strict, b_col[:half] * d00 * kk[:half, :half], 0.0)
        l11 = jnp.where(strict, b_col[half:] * d11 * kk[half:, half:], 0.0)
        l10 = (b_col[half:] * d10 * kk[half:, :half]).astype(BF16)
        s00 = (d00 * qk[:half, :half]).astype(BF16)
        s1 = jnp.concatenate(
            [(d10 * qk[half:, :half]).astype(BF16), (d11 * qk[half:, half:]).astype(BF16)], axis=1
        )
        v = normed[:, pl.ds(pl.multiple_of(step * (GROUP * 128) + h * 128, 128), 128)].astype(F32)
        e_col = jnp.exp(c_col)
        right = jnp.concatenate([b_col * v, (b_col * e_col) * kf], axis=1)
        carried_t = (ktf * jnp.exp(c_end - c_row)).astype(BF16)
        heads.append((l00, l11, l10, s00, s1, right, carried_t, e_col * qf, jnp.exp(c_end)))

    inverses = base_inverses([c for hd in heads for c in hd[:2]])
    couplings = [c.astype(BF16) for hd in heads for c in hd[:2]]
    m = BASE
    while m < half:
        inverses = [merge(x, c, m) for x, c in zip(inverses, couplings)]
        m *= 2

    eye = ri == ci
    for h in range(GROUP):
        l00, l11, l10, s00, s1, right, carried_t, eq, total = heads[h]
        top = mm(inverses[2 * h], right[:half].astype(BF16)).astype(BF16)
        rest = (right[half:].astype(BF16).astype(F32) - mm(l10, top)).astype(BF16)
        low = mm(inverses[2 * h + 1], rest).astype(BF16)
        solved = jnp.concatenate([top, low], axis=0)
        pair = mm(carried_t, solved)
        ts_ref[h, 0] = (jnp.where(eye, total, 0.0) - pair[:, 128:]).astype(BF16)
        ts_ref[h, 1] = pair[:, :128].astype(BF16)
        out0 = mm(s00, top)
        out1 = mm(s1, solved)
        at = h * 128
        loc_ref[:half, at : at + 128] = out0[:, :128]
        loc_ref[half:, at : at + 128] = out1[:, :128]
        qr_ref[:half, at : at + 128] = (eq[:half] - out0[:, 128:]).astype(BF16)
        qr_ref[half:, at : at + 128] = (eq[half:] - out1[:, 128:]).astype(BF16)


def local_terms(x, weight, gain_in, log_decay, write_rate):
    tokens, width = x.shape
    heads = log_decay.shape[0]
    steps = heads // GROUP
    wcols = GROUP // 2 * 128
    return pl.pallas_call(
        local_kernel,
        grid=(steps,),
        in_specs=[
            pl.BlockSpec((tokens, width), lambda s: (0, 0)),
            pl.BlockSpec((1, width), lambda s: (0, 0)),
            pl.BlockSpec((heads, tokens), lambda s: (0, 0)),
            pl.BlockSpec((heads, tokens), lambda s: (0, 0)),
            pl.BlockSpec((width, wcols), lambda s: (0, s)),
            pl.BlockSpec((width, wcols), lambda s: (0, s + steps)),
        ],
        out_specs=[
            pl.BlockSpec((GROUP, 2, 128, 128), lambda s: (s, 0, 0, 0)),
            pl.BlockSpec((tokens, GROUP * 128), lambda s: (0, s)),
            pl.BlockSpec((tokens, GROUP * 128), lambda s: (0, s)),
        ],
        out_shape=[
            jax.ShapeDtypeStruct((heads, 2, 128, 128), BF16),
            jax.ShapeDtypeStruct((tokens, heads * 128), BF16),
            jax.ShapeDtypeStruct((tokens, heads * 128), F32),
        ],
        scratch_shapes=[
            pltpu.VMEM((tokens, width), BF16),
            pltpu.VMEM((steps, 2 * GROUP, tokens), F32),
            pltpu.VMEM((steps, tokens, 2 * GROUP), F32),
        ],
        compiler_params=pltpu.CompilerParams(vmem_limit_bytes=40 * 1024 * 1024),
        name="local_terms",
    )(x, gain_in, log_decay, write_rate, weight, weight)


def prefix_kernel(ts_ref, out_ref):
    shards = ts_ref.shape[0]
    out_ref[0] = jnp.zeros(out_ref.shape[1:], BF16)
    state = ts_ref[0, 1].astype(F32)
    out_ref[1] = state.astype(BF16)
    for p in range(1, shards - 1):
        hi = state.astype(BF16)
        low = (state - hi.astype(F32)).astype(BF16)
        prod = mm(ts_ref[p, 0], jnp.concatenate([hi, low], axis=1))
        state = prod[:, :128] + prod[:, 128:] + ts_ref[p, 1].astype(F32)
        out_ref[p + 1] = state.astype(BF16)


def prefix_states(ts):
    return pl.pallas_call(
        prefix_kernel,
        out_shape=jax.ShapeDtypeStruct((ts.shape[0], 128, 128), BF16),
        compiler_params=pltpu.CompilerParams(vmem_limit_bytes=16 * 1024 * 1024),
        name="prefix_states",
    )(ts)


def finish_kernel(qr_ref, loc_ref, state_ref, x_ref, gain_ref, out_ref):
    gain = gain_ref[...]
    for h in range(state_ref.shape[0]):
        at = h * 128
        mixed = mm(qr_ref[:, at : at + 128], state_ref[h]) + loc_ref[:, at : at + 128]
        scaled = mixed * lax.rsqrt(jnp.mean(mixed * mixed, axis=-1, keepdims=True) + EPS) * gain
        branch = scaled.astype(BF16).astype(F32)
        out_ref[:, at : at + 128] = (x_ref[:, at : at + 128].astype(F32) + branch).astype(BF16)


def finish(qr, loc, states, x, gain_out):
    tokens, width = x.shape
    heads = states.shape[0]
    per = 4
    block = pl.BlockSpec((tokens, per * 128), lambda s: (0, s))
    return pl.pallas_call(
        finish_kernel,
        grid=(heads // per,),
        in_specs=[
            block,
            block,
            pl.BlockSpec((per, 128, 128), lambda s: (s, 0, 0)),
            block,
            pl.BlockSpec((1, 128), lambda s: (0, 0)),
        ],
        out_specs=block,
        out_shape=jax.ShapeDtypeStruct((tokens, width), BF16),
        compiler_params=pltpu.CompilerParams(vmem_limit_bytes=24 * 1024 * 1024),
        name="finish",
    )(qr, loc, states, x, gain_out)


def on_device(layer_input, qk_weight, norm_gain, out_gain, log_decay, write_rate):
    x = layer_input[0]
    ts, qr, loc = local_terms(x, qk_weight[0], norm_gain, log_decay[0], write_rate[0])
    owned = lax.all_to_all(ts, "ctx", 0, 0)
    starts = lax.all_to_all(prefix_states(owned), "ctx", 0, 0)
    done = finish(qr, loc, starts, x, out_gain)
    n = lax.axis_size("section")
    return lax.ppermute(done, "section", [(i, (i + 1) % n) for i in range(n)])[None]


def solution(mesh):
    in_specs = (
        P("section", "ctx", None),
        P("section", None, None),
        P("section", None),
        P("section", None),
        P("section", None, "ctx"),
        P("section", None, "ctx"),
    )
    out_specs = P("section", "ctx", None)
    return jax.shard_map(
        on_device, mesh=mesh, in_specs=in_specs, out_specs=out_specs, check_vma=False
    )
```

```python
import jax
import jax.numpy as jnp
from jax import lax
from jax.experimental import pallas as pl
from jax.experimental.pallas import tpu as pltpu
from jax.sharding import PartitionSpec as P

F32 = jnp.float32
BF16 = jnp.bfloat16
EPS = 1e-6
HALF = 128
BASE = 16
GROUP = 8
XS = 4
VMEM = pl.BlockSpec(memory_space=pltpu.VMEM)


def in_hbm(array):
    return pltpu.with_memory_space_constraint(array, pltpu.HBM)


def place():
    at = lax.axis_index("ctx")
    return at % 2, at // 2 % XS


def mm(a, b):
    return jnp.dot(a, b, preferred_element_type=F32)


def iota(shape, dim):
    return lax.broadcasted_iota(jnp.int32, shape, dim)


def base_inverses(couplings):
    lanes = HALF
    count = len(couplings)
    blocks = lanes // BASE
    lane = iota((BASE, lanes), 1)
    packed = []
    for c in couplings:
        d = jnp.zeros((BASE, lanes), F32)
        for blk in range(blocks):
            d = jnp.where(lane // BASE == blk, c[blk * BASE : (blk + 1) * BASE, :], d)
        packed.append(d)
    d = jnp.concatenate(packed, axis=0)
    rows = count * BASE
    lane_all = iota((rows, lanes), 1)
    x = jnp.where(iota((rows, lanes), 0) % BASE == lane_all % BASE, 1.0, 0.0).astype(F32)
    x = x.reshape(count, BASE, lanes)
    for j in range(BASE - 1):
        spread = jnp.take_along_axis(d, lane_all // BASE * BASE + j, axis=1)
        x = x - spread.reshape(count, BASE, lanes) * x[:, j : j + 1, :]
    full = []
    for n in range(count):
        full.append(
            jnp.concatenate(
                [jnp.where(lane // BASE == blk, x[n], 0.0) for blk in range(blocks)], axis=0
            ).astype(BF16)
        )
    return full


def merge(x, coupling, m):
    size = x.shape[0]
    pairs = size // (2 * m)
    lane = iota((m, size), 1)
    left, odd = [], []
    for p in range(pairs):
        at = (2 * p + 1) * m
        left.append(jnp.where(lane // m == 2 * p, coupling[at : at + m, :], jnp.zeros((), BF16)))
        odd.append(x[at : at + m, :])
    y = mm(jnp.concatenate(left, axis=0), x).astype(BF16)
    spread = []
    for p in range(pairs):
        spread += [jnp.zeros((m, size), BF16), y[p * m : (p + 1) * m, :]]
    z = mm(jnp.concatenate(odd, axis=0), jnp.concatenate(spread, axis=0)).astype(BF16)
    out = []
    for p in range(pairs):
        out += [x[2 * p * m : (2 * p + 1) * m, :], odd[p] - z[p * m : (p + 1) * m, :]]
    return jnp.concatenate(out, axis=0)


def fetch(pairs, sems):
    copies = [pltpu.make_async_copy(a, b, sems.at[n]) for n, (a, b) in enumerate(pairs)]
    for copy in copies:
        copy.start()
    return copies


def local_kernel(
    x_hbm, gain_hbm, decay_hbm, rate_hbm, w_hbm, ts_ref, qr_ref, loc_ref, xbuf,
    gains, logs_buf, rates_buf, wbuf, normed, sems,
):
    tokens, width = xbuf.shape
    steps = wbuf.shape[0]
    wcols = wbuf.shape[3]
    half = HALF
    pairs = [(x_hbm, xbuf), (gain_hbm, gains), (decay_hbm, logs_buf), (rate_hbm, rates_buf)]
    for s in range(steps):
        pairs.append((w_hbm.at[:, pl.ds(s * wcols, wcols)], wbuf.at[s, 0]))
        pairs.append((w_hbm.at[:, pl.ds(width // 2 + s * wcols, wcols)], wbuf.at[s, 1]))
    copies = fetch(pairs, sems)

    ri = iota((half, half), 0)
    ci = iota((half, half), 1)
    incl = ci <= ri
    strict = ci < ri
    eye = ri == ci

    copies[2].wait()
    copies[3].wait()
    upto = (iota((tokens, tokens), 0) <= iota((tokens, tokens), 1)).astype(BF16)
    logs = logs_buf[...]
    hi = logs.astype(BF16)
    rest = logs - hi.astype(F32)
    mid = rest.astype(BF16)
    low = (rest - mid.astype(F32)).astype(BF16)
    cumul = mm(hi, upto) + (mm(mid, upto) + mm(low, upto))
    cols = jnp.concatenate([cumul, rates_buf[...]], axis=0).T
    heads_all = cumul.shape[0]
    core, _ = place()

    copies[0].wait()
    copies[1].wait()
    for r in range(0, tokens, 64):
        xf = xbuf[r : r + 64, :].astype(F32)
        normed[r : r + 64, :] = (
            xf * lax.rsqrt(jnp.mean(xf * xf, axis=-1, keepdims=True) + EPS) * gains[...]
        ).astype(BF16)

    def project(s):
        copies[4 + 2 * s].wait()
        copies[5 + 2 * s].wait()
        return mm(normed[...], wbuf[s, 0]), mm(normed[...], wbuf[s, 1])

    def prepare(s, pq, pk):
        heads = []
        for h in range(GROUP):
            at = h // 2 * 128
            if h % 2 == 0:
                q = pq[:, at : at + 128].astype(BF16)
                raw = pk[:, at : at + 128]
                k = (raw * lax.rsqrt(jnp.sum(raw * raw, axis=-1, keepdims=True) + EPS)).astype(BF16)
                kt = k.T
                g0 = mm(jnp.concatenate([k[:half], q[:half]], axis=0), kt[:, :half])
                g1 = mm(jnp.concatenate([k[half:], q[half:]], axis=0), kt)
                kf = k.astype(F32)
                qf = q.astype(F32)
                ktf = kt.astype(F32)
            n = s * GROUP + h
            c = jnp.broadcast_to(cols[:, n : n + 1], (tokens, half))
            b = jnp.broadcast_to(cols[:, heads_all + n : heads_all + n + 1], (tokens, half))
            c_row = cumul[n : n + 1, :]
            c_end = c_row[:, tokens - 1 : tokens]
            c_mid = c_row[:, half - 1 : half]
            d00 = jnp.where(incl, jnp.exp(c[:half] - c_row[:, :half]), 0.0)
            d11 = jnp.where(incl, jnp.exp(c[half:] - c_row[:, half:]), 0.0)
            d10 = jnp.exp(c[half:] - c_mid) * jnp.exp(c_mid - c_row[:, :half])
            l00 = jnp.where(strict, b[:half] * d00 * g0[:half], 0.0)
            l11 = jnp.where(strict, b[half:] * d11 * g1[:half, half:], 0.0)
            l10 = (b[half:] * d10 * g1[:half, :half]).astype(BF16)
            s00 = (d00 * g0[half:]).astype(BF16)
            s1 = jnp.concatenate(
                [(d10 * g1[half:, :half]).astype(BF16), (d11 * g1[half:, half:]).astype(BF16)],
                axis=1,
            )
            v = normed[:, n * 128 : n * 128 + 128].astype(F32)
            e = jnp.exp(c)
            right = jnp.concatenate([(b * v).astype(BF16), (b * e * kf).astype(BF16)], axis=1)
            carried_t = (ktf * jnp.exp(c_end - c_row)).astype(BF16)
            heads.append((l00, l11, l10, s00, s1, right, carried_t, e * qf, jnp.exp(c_end)))
        return heads

    def invert(heads):
        inverses = base_inverses([c for hd in heads for c in hd[:2]])
        couplings = [c.astype(BF16) for hd in heads for c in hd[:2]]
        m = BASE
        while m < half:
            inverses = [merge(x, c, m) for x, c in zip(inverses, couplings)]
            m *= 2
        return inverses

    def emit(s, heads, inverses):
        for h in range(GROUP):
            l00, l11, l10, s00, s1, right, carried_t, eq, total = heads[h]
            top = mm(inverses[2 * h], right[:half]).astype(BF16)
            rest = (right[half:].astype(F32) - mm(l10, top)).astype(BF16)
            low = mm(inverses[2 * h + 1], rest).astype(BF16)
            solved = jnp.concatenate([top, low], axis=0)
            pair = mm(carried_t, solved)
            n = s * GROUP + h
            slot = core if n < heads_all // 2 else 1 - core
            ts_ref[slot, n % (heads_all // 2), 0] = (
                jnp.where(eye, total, 0.0) - pair[:, 128:]
            ).astype(BF16)
            ts_ref[slot, n % (heads_all // 2), 1] = pair[:, :128].astype(BF16)
            out0 = mm(s00, top)
            out1 = mm(s1, solved)
            at = n * 128
            loc_ref[:half, at : at + 128] = out0[:, :128].astype(loc_ref.dtype)
            loc_ref[half:, at : at + 128] = out1[:, :128].astype(loc_ref.dtype)
            qr_ref[:half, at : at + 128] = (eq[:half] - out0[:, 128:]).astype(BF16)
            qr_ref[half:, at : at + 128] = (eq[half:] - out1[:, 128:]).astype(BF16)

    pq, pk = project(0)
    for s in range(steps):
        heads = prepare(s, pq, pk)
        if s + 1 < steps:
            pq, pk = project(s + 1)
        emit(s, heads, invert(heads))


def local_terms(x, weight, gain_in, log_decay, write_rate):
    tokens, width = x.shape
    heads = log_decay.shape[0]
    steps = heads // GROUP
    wcols = GROUP // 2 * 128
    return pl.pallas_call(
        local_kernel,
        in_specs=[pl.BlockSpec(memory_space=pltpu.HBM)] * 5,
        out_specs=[VMEM] * 4,
        out_shape=[
            jax.ShapeDtypeStruct((2, heads // 2, 2, 128, 128), BF16),
            jax.ShapeDtypeStruct((tokens, heads * 128), BF16),
            jax.ShapeDtypeStruct((tokens, heads * 128), BF16),
            jax.ShapeDtypeStruct((tokens, width), BF16),
        ],
        scratch_shapes=[
            pltpu.VMEM((1, width), F32),
            pltpu.VMEM((heads, tokens), F32),
            pltpu.VMEM((heads, tokens), F32),
            pltpu.VMEM((steps, 2, width, wcols), BF16),
            pltpu.VMEM((tokens, width), BF16),
            pltpu.SemaphoreType.DMA((4 + 2 * steps,)),
        ],
        compiler_params=pltpu.CompilerParams(vmem_limit_bytes=40 * 1024 * 1024),
        name="local_terms",
    )(*[in_hbm(a) for a in (x, gain_in, log_decay, write_rate, weight)])


def small_call(kernel, outs, args, name, scratch=()):
    return pl.pallas_call(
        kernel,
        in_specs=[VMEM] * len(args),
        out_specs=[VMEM] * len(outs),
        out_shape=[jax.ShapeDtypeStruct(shape, BF16) for shape in outs],
        scratch_shapes=list(scratch),
        compiler_params=pltpu.CompilerParams(vmem_limit_bytes=16 * 1024 * 1024),
        name=name,
    )(*args)


def compose_kernel(keep, other, *outs):
    core, chip = place()
    first = core == 0
    for shift, out in enumerate(outs):
        for i in range(out.shape[0]):
            h = (chip + shift) % XS * out.shape[0] + i
            mine, theirs = keep[h], other[h]
            early = jnp.where(first, mine, theirs)
            late = jnp.where(first, theirs, mine)
            prod = mm(late[0], jnp.concatenate([early[0], early[1]], axis=1))
            out[i, 0] = prod[:, :128].astype(BF16)
            out[i, 1] = (prod[:, 128:] + late[1].astype(F32)).astype(BF16)


def advance(trans, state, extra):
    hi = state.astype(BF16)
    low = (state - hi.astype(F32)).astype(BF16)
    prod = mm(trans, jnp.concatenate([hi, low], axis=1))
    return prod[:, :128] + prod[:, 128:] + extra.astype(F32)


def total_kernel(*refs):
    parts, (ordered, total) = refs[:XS], refs[XS:]
    _, chip = place()
    for shift, part in enumerate(parts):
        ordered[(chip + XS - shift) % XS] = part[...]
    for i in range(total.shape[0]):
        state = ordered[0, i, 1].astype(F32)
        for j in range(1, XS):
            state = advance(ordered[j, i, 0], state, ordered[j, i, 1])
        total[i] = state.astype(BF16)


def starts_kernel(ordered, before, *refs):
    outs, scratch = refs[:XS], refs[XS]
    _, chip = place()
    for i in range(before.shape[0]):
        state = before[i].astype(F32)
        for j in range(XS):
            scratch[(j + XS - chip) % XS, i] = state.astype(BF16)
            if j + 1 < XS:
                state = advance(ordered[j, i, 0], state, ordered[j, i, 1])
    for shift, out in enumerate(outs):
        out[...] = scratch[shift]


def pair_kernel(*refs):
    parts, (keep, other, mine, theirs) = refs[:XS], refs[XS:]
    core, chip = place()
    first = core == 0
    for shift, part in enumerate(parts):
        for i in range(part.shape[0]):
            h = (chip + XS - shift) % XS * part.shape[0] + i
            early = jnp.where(first, keep[h], other[h])
            start = part[i]
            after = (mm(early[0], start) + early[1].astype(F32)).astype(BF16)
            mine[h] = jnp.where(first, start, after)
            theirs[h] = jnp.where(first, after, start)


def finish_kernel(qr_ref, loc_ref, mine, got, x_ref, gain_ref, out_ref):
    gain = gain_ref[...]
    core, _ = place()
    half = mine.shape[0]
    for h in range(2 * half):
        at = h * 128
        state = jnp.where(core == h // half, mine[h % half], got[h % half])
        mixed = mm(qr_ref[:, at : at + 128], state) + loc_ref[:, at : at + 128].astype(F32)
        scaled = mixed * lax.rsqrt(jnp.mean(mixed * mixed, axis=-1, keepdims=True) + EPS) * gain
        branch = scaled.astype(BF16).astype(F32)
        out_ref[:, at : at + 128] = (x_ref[:, at : at + 128].astype(F32) + branch).astype(BF16)


def swap_cores(array):
    return lax.ppermute(array, "ctx", [(i, i ^ 1) for i in range(lax.axis_size("ctx"))])


def along_x(array, shift):
    pairs = []
    for i in range(lax.axis_size("ctx")):
        row, chip, core = i // (2 * XS), i // 2 % XS, i % 2
        pairs.append((i, (row * XS + (chip + shift) % XS) * 2 + core))
    return lax.ppermute(array, "ctx", pairs)


def start_states(keep, send):
    half = keep.shape[0]
    per = half // XS
    other = swap_cores(send)
    parts = small_call(compose_kernel, [(per, 2, 128, 128)] * XS, (keep, other), "compose")
    parts = [parts[0]] + [along_x(parts[r], r) for r in range(1, XS)]
    ordered, total = small_call(
        total_kernel, [(XS, per, 2, 128, 128), (per, 128, 128)], parts, "row_total"
    )
    row = 2 * XS
    before = lax.ppermute(total, "ctx", [(i, i + row) for i in range(row)])
    starts = small_call(
        starts_kernel,
        [(per, 128, 128)] * XS,
        (ordered, before),
        "row_starts",
        [pltpu.VMEM((XS, per, 128, 128), BF16)],
    )
    starts = [starts[0]] + [along_x(starts[r], r) for r in range(1, XS)]
    mine, theirs = small_call(
        pair_kernel, [(half, 128, 128)] * 2, (*starts, keep, other), "pair_starts"
    )
    return mine, swap_cores(theirs)


def on_device(layer_input, qk_weight, norm_gain, out_gain, log_decay, write_rate):
    x = layer_input[0]
    ts, qr, loc, kept = local_terms(x, qk_weight[0], norm_gain, log_decay[0], write_rate[0])
    mine, got = start_states(ts[0], ts[1])
    done = small_call(finish_kernel, [x.shape], (qr, loc, mine, got, kept, out_gain), "finish")[0]
    n = lax.axis_size("section")
    return lax.ppermute(done, "section", [(i, (i + 1) % n) for i in range(n)])[None]


def solution(mesh):
    in_specs = (
        P("section", "ctx", None),
        P("section", None, None),
        P("section", None),
        P("section", None),
        P("section", None, "ctx"),
        P("section", None, "ctx"),
    )
    out_specs = P("section", "ctx", None)
    return jax.shard_map(
        on_device, mesh=mesh, in_specs=in_specs, out_specs=out_specs, check_vma=False
    )
```

```python
import functools

import jax
import jax.numpy as jnp
from jax import lax
from jax.experimental import pallas as pl
from jax.experimental.pallas import tpu as pltpu
from jax.sharding import PartitionSpec as P

F32 = jnp.float32
BF16 = jnp.bfloat16
EPS = 1e-6
HALF = 128
BASE = 16
GROUP = 8
XS = 4
VMEM = pl.BlockSpec(memory_space=pltpu.VMEM)


def in_hbm(array):
    return pltpu.with_memory_space_constraint(array, pltpu.HBM)


def place():
    at = lax.axis_index("ctx")
    return at % 2, at // 2 % XS


def mm(a, b):
    return jnp.dot(a, b, preferred_element_type=F32)


def iota(shape, dim):
    return lax.broadcasted_iota(jnp.int32, shape, dim)


def base_inverses(couplings):
    lanes = HALF
    count = len(couplings)
    blocks = lanes // BASE
    lane = iota((BASE, lanes), 1)
    packed = []
    for c in couplings:
        d = jnp.zeros((BASE, lanes), F32)
        for blk in range(blocks):
            d = jnp.where(lane // BASE == blk, c[blk * BASE : (blk + 1) * BASE, :], d)
        packed.append(d)
    d = jnp.concatenate(packed, axis=0)
    rows = count * BASE
    lane_all = iota((rows, lanes), 1)
    x = jnp.where(iota((rows, lanes), 0) % BASE == lane_all % BASE, 1.0, 0.0).astype(F32)
    x = x.reshape(count, BASE, lanes)
    for j in range(BASE - 1):
        spread = jnp.take_along_axis(d, lane_all // BASE * BASE + j, axis=1)
        x = x - spread.reshape(count, BASE, lanes) * x[:, j : j + 1, :]
    full = []
    for n in range(count):
        full.append(
            jnp.concatenate(
                [jnp.where(lane // BASE == blk, x[n], 0.0) for blk in range(blocks)], axis=0
            ).astype(BF16)
        )
    return full


def merge(inverses, couplings, m):
    size = HALF
    pairs = size // (2 * m)
    lane = iota((m, size), 1)
    odd_at = [(2 * p + 1) * m for p in range(pairs)]
    left = [
        jnp.concatenate(
            [
                jnp.where(lane // m == 2 * p, c[at : at + m, :], jnp.zeros((), BF16))
                for p, at in enumerate(odd_at)
            ],
            axis=0,
        )
        for c in couplings
    ]
    middle = [mm(a, x).astype(BF16) for a, x in zip(left, inverses)]
    blank = jnp.zeros((m, size), BF16)
    spread = [
        jnp.concatenate(
            [part for p in range(pairs) for part in (blank, y[p * m : (p + 1) * m, :])], axis=0
        )
        for y in middle
    ]
    odd = [jnp.concatenate([x[at : at + m, :] for at in odd_at], axis=0) for x in inverses]
    lower = [mm(a, y).astype(BF16) for a, y in zip(odd, spread)]
    return [
        jnp.concatenate(
            [
                part
                for p, at in enumerate(odd_at)
                for part in (x[at - m : at, :], (o - z)[p * m : (p + 1) * m, :])
            ],
            axis=0,
        )
        for x, o, z in zip(inverses, odd, lower)
    ]


def split3(value):
    hi = value.astype(BF16)
    rest = value - hi.astype(F32)
    mid = rest.astype(BF16)
    return hi, mid, (rest - mid.astype(F32)).astype(BF16)


def fetch(pairs, sems):
    copies = [pltpu.make_async_copy(a, b, sems.at[n]) for n, (a, b) in enumerate(pairs)]
    for copy in copies:
        copy.start()
    return copies


def local_kernel(
    x_hbm, gain_hbm, decay_hbm, rate_hbm, w_hbm,
    keep_ref, send_ref, near_ref, far_ref, xbuf,
    gains, logs_buf, rates_buf, wbuf, normed, sems,
):
    tokens, width = xbuf.shape
    steps = wbuf.shape[0]
    wcols = wbuf.shape[3]
    half = HALF
    heads_all = logs_buf.shape[0]
    mid_head = heads_all // 2
    core, _ = place()
    here = pl.multiple_of(core * mid_head, mid_head)
    there = pl.multiple_of((1 - core) * mid_head, mid_head)
    pairs = [(x_hbm, xbuf), (gain_hbm, gains)]
    for at, frm in ((0, here), (mid_head, there)):
        pairs.append((decay_hbm.at[pl.ds(frm, mid_head)], logs_buf.at[pl.ds(at, mid_head)]))
        pairs.append((rate_hbm.at[pl.ds(frm, mid_head)], rates_buf.at[pl.ds(at, mid_head)]))
    w_at = len(pairs)
    for s in range(steps):
        frm = pl.multiple_of((s * wcols + core * (width // 4)) % (width // 2), 128)
        pairs.append((w_hbm.at[:, pl.ds(frm, wcols)], wbuf.at[s, 0]))
        frm = pl.multiple_of(width // 2 + frm, 128)
        pairs.append((w_hbm.at[:, pl.ds(frm, wcols)], wbuf.at[s, 1]))
    copies = fetch(pairs, sems)

    ri = iota((half, half), 0)
    ci = iota((half, half), 1)
    incl = ci <= ri
    strict = ci < ri
    eye = ri == ci

    for copy in copies[2:w_at]:
        copy.wait()
    upto = (iota((tokens, tokens), 0) <= iota((tokens, tokens), 1)).astype(BF16)
    hi, mid, low = split3(logs_buf[...])
    cumul = mm(hi, upto) + (mm(mid, upto) + mm(low, upto))
    cols = jnp.concatenate([cumul, rates_buf[...]], axis=0).T

    copies[0].wait()
    copies[1].wait()
    for r in range(0, tokens, 64):
        xf = xbuf[r : r + 64, :].astype(F32)
        normed[r : r + 64, :] = (
            xf * lax.rsqrt(jnp.mean(xf * xf, axis=-1, keepdims=True) + EPS) * gains[...]
        ).astype(BF16)

    def project(s):
        copies[w_at + 2 * s].wait()
        copies[w_at + 1 + 2 * s].wait()
        return mm(normed[...], wbuf[s, 0]), mm(normed[...], wbuf[s, 1])

    def prepare(s, pq, pk):
        heads = []
        for h in range(GROUP):
            at = h // 2 * 128
            if h % 2 == 0:
                q = pq[:, at : at + 128].astype(BF16)
                raw = pk[:, at : at + 128]
                k = (raw * lax.rsqrt(jnp.sum(raw * raw, axis=-1, keepdims=True) + EPS)).astype(BF16)
                kt = k.T
                g0 = mm(jnp.concatenate([k[:half], q[:half]], axis=0), kt[:, :half])
                g1 = mm(jnp.concatenate([k[half:], q[half:]], axis=0), kt)
                kf = k.astype(F32)
                qf = q.astype(F32)
                ktf = kt.astype(F32)
            n = s * GROUP + h
            c = jnp.broadcast_to(cols[:, n : n + 1], (tokens, half))
            b = jnp.broadcast_to(cols[:, heads_all + n : heads_all + n + 1], (tokens, half))
            c_row = cumul[n : n + 1, :]
            c_end = c_row[:, tokens - 1 : tokens]
            c_mid = c_row[:, half - 1 : half]
            d00 = jnp.where(incl, jnp.exp(c[:half] - c_row[:, :half]), 0.0)
            d11 = jnp.where(incl, jnp.exp(c[half:] - c_row[:, half:]), 0.0)
            d10 = jnp.exp(c[half:] - c_mid) * jnp.exp(c_mid - c_row[:, :half])
            l00 = jnp.where(strict, b[:half] * d00 * g0[:half], 0.0)
            l11 = jnp.where(strict, b[half:] * d11 * g1[:half, half:], 0.0)
            l10 = (b[half:] * d10 * g1[:half, :half]).astype(BF16)
            s00 = (d00 * g0[half:]).astype(BF16)
            s1 = jnp.concatenate(
                [(d10 * g1[half:, :half]).astype(BF16), (d11 * g1[half:, half:]).astype(BF16)],
                axis=1,
            )
            v_at = pl.multiple_of((n * 128 + core * (width // 2)) % width, 128)
            v = normed[:, pl.ds(v_at, 128)].astype(F32)
            e = jnp.exp(c)
            right = jnp.concatenate([(b * v).astype(BF16), (b * e * kf).astype(BF16)], axis=1)
            carried_t = (ktf * jnp.exp(c_end - c_row)).astype(BF16)
            heads.append((l00, l11, l10, s00, s1, right, carried_t, e * qf, jnp.exp(c_end)))
        return heads

    def invert(heads):
        inverses = base_inverses([c for hd in heads for c in hd[:2]])
        couplings = [c.astype(BF16) for hd in heads for c in hd[:2]]
        m = BASE
        while m < half:
            inverses = merge(inverses, couplings, m)
            m *= 2
        return inverses

    def emit(s, heads, inverses):
        tops = [mm(x, hd[5][:half]).astype(BF16) for x, hd in zip(inverses[::2], heads)]
        rests = [
            (hd[5][half:].astype(F32) - mm(hd[2], top)).astype(BF16) for hd, top in zip(heads, tops)
        ]
        lows = [mm(x, rest).astype(BF16) for x, rest in zip(inverses[1::2], rests)]
        for h in range(GROUP):
            _, _, _, s00, s1, _, carried_t, eq, total = heads[h]
            top = tops[h]
            solved = jnp.concatenate([top, lows[h]], axis=0)
            pair = mm(carried_t, solved)
            n = s * GROUP + h
            pairs_ref, rows_ref = (keep_ref, near_ref) if n < mid_head else (send_ref, far_ref)
            p = n % mid_head
            pairs_ref[p, 0] = (jnp.where(eye, total, 0.0) - pair[:, 128:]).astype(BF16)
            pairs_ref[p, 1] = pair[:, :128].astype(BF16)
            out0 = mm(s00, top)
            out1 = mm(s1, solved)
            at = p * 128
            rows_ref[0, :half, at : at + 128] = (eq[:half] - out0[:, 128:]).astype(BF16)
            rows_ref[0, half:tokens, at : at + 128] = (eq[half:] - out1[:, 128:]).astype(BF16)
            rows_ref[1, :half, at : at + 128] = out0[:, :128].astype(BF16)
            rows_ref[1, half:tokens, at : at + 128] = out1[:, :128].astype(BF16)

    pq, pk = project(0)
    for s in range(steps):
        heads = prepare(s, pq, pk)
        if s + 1 < steps:
            pq, pk = project(s + 1)
        emit(s, heads, invert(heads))


def local_terms(x, weight, gain_in, log_decay, write_rate):
    tokens, width = x.shape
    heads = log_decay.shape[0]
    steps = heads // GROUP
    wcols = GROUP // 2 * 128
    return pl.pallas_call(
        local_kernel,
        in_specs=[pl.BlockSpec(memory_space=pltpu.HBM)] * 5,
        out_specs=[VMEM] * 5,
        out_shape=[
            jax.ShapeDtypeStruct((heads // 2, 2, 128, 128), BF16),
            jax.ShapeDtypeStruct((heads // 2, 2, 128, 128), BF16),
            jax.ShapeDtypeStruct((2, tokens, width // 2), BF16),
            jax.ShapeDtypeStruct((2, tokens, width // 2), BF16),
            jax.ShapeDtypeStruct((tokens, width), BF16),
        ],
        scratch_shapes=[
            pltpu.VMEM((1, width), F32),
            pltpu.VMEM((heads, tokens), F32),
            pltpu.VMEM((heads, tokens), F32),
            pltpu.VMEM((steps, 2, width, wcols), BF16),
            pltpu.VMEM((tokens, width), BF16),
            pltpu.SemaphoreType.DMA((6 + 2 * steps,)),
        ],
        compiler_params=pltpu.CompilerParams(vmem_limit_bytes=40 * 1024 * 1024),
        cost_estimate=pl.CostEstimate(
            flops=16_000_000_000, bytes_accessed=16_000_000, transcendentals=2_000_000
        ),
        name="local_terms",
    )(*[in_hbm(a) for a in (x, gain_in, log_decay, write_rate, weight)])


def small_call(kernel, outs, args, name, scratch=()):
    return pl.pallas_call(
        kernel,
        in_specs=[VMEM] * len(args),
        out_specs=[VMEM] * len(outs),
        out_shape=[jax.ShapeDtypeStruct(shape, BF16) for shape in outs],
        scratch_shapes=list(scratch),
        compiler_params=pltpu.CompilerParams(vmem_limit_bytes=16 * 1024 * 1024),
        name=name,
    )(*args)


def compose_kernel(keep, other, *outs):
    core, chip = place()
    first = core == 0
    for shift, out in enumerate(outs):
        for i in range(out.shape[0]):
            h = (chip + shift) % XS * out.shape[0] + i
            mine, theirs = keep[h], other[h]
            early = jnp.where(first, mine, theirs)
            late = jnp.where(first, theirs, mine)
            prod = mm(late[0], jnp.concatenate([early[0], early[1]], axis=1))
            out[i, 0] = prod[:, :128].astype(BF16)
            out[i, 1] = (prod[:, 128:] + late[1].astype(F32)).astype(BF16)


def advance(trans, state, extra):
    hi = state.astype(BF16)
    low = (state - hi.astype(F32)).astype(BF16)
    prod = mm(trans, jnp.concatenate([hi, low], axis=1))
    return prod[:, :128] + prod[:, 128:] + extra.astype(F32)


def total_kernel(*refs):
    parts, (ordered, total) = refs[:XS], refs[XS:]
    _, chip = place()
    for shift, part in enumerate(parts):
        ordered[(chip + XS - shift) % XS] = part[...]
    for i in range(total.shape[0]):
        state = ordered[0, i, 1].astype(F32)
        for j in range(1, XS):
            state = advance(ordered[j, i, 0], state, ordered[j, i, 1])
        total[i] = state.astype(BF16)


def starts_kernel(ordered, before, *refs):
    outs, scratch = refs[:XS], refs[XS]
    _, chip = place()
    for i in range(before.shape[0]):
        state = before[i].astype(F32)
        for j in range(XS):
            scratch[(j + XS - chip) % XS, i] = state.astype(BF16)
            if j + 1 < XS:
                state = advance(ordered[j, i, 0], state, ordered[j, i, 1])
    for shift, out in enumerate(outs):
        out[...] = scratch[shift]


def finish_head(rows_ref, rows_at, state, x_ref, x_at, gain):
    cols = pl.ds(pl.multiple_of(rows_at, 128), 128)
    mixed = mm(rows_ref[0, :, cols], state) + rows_ref[1, :, cols].astype(F32)
    scaled = mixed * lax.rsqrt(jnp.mean(mixed * mixed, axis=-1, keepdims=True) + EPS) * gain
    rows = x_ref[:, pl.ds(pl.multiple_of(x_at, 128), 128)].astype(F32)
    return (rows + scaled.astype(BF16).astype(F32)).astype(BF16)


def looked_after(parts, shifts, keep, other):
    core, chip = place()
    first = core == 0
    at = 0
    for shift, part in zip(shifts, parts):
        for i in range(part.shape[0]):
            h = (chip + XS - shift) % XS * part.shape[0] + i
            early = jnp.where(first, keep[h], other[h])
            start = part[i]
            after = (mm(early[0], start) + early[1].astype(F32)).astype(BF16)
            yield at, h, jnp.where(first, start, after), jnp.where(first, after, start)
            at += 128


def near_heads(parts, shifts, keep, other, near, x_ref, gain_ref, out_ref):
    core, _ = place()
    mid = x_ref.shape[1] // 2
    for at, h, mine, _ in looked_after(parts, shifts, keep, other):
        out_ref[:, at : at + 128] = finish_head(
            near, h * 128, mine, x_ref, core * mid + h * 128, gain_ref[...]
        )


def near_own_kernel(part, *refs):
    near_heads([part], [0], *refs)


def near_rest_kernel(*refs):
    near_heads(refs[: XS - 1], range(1, XS), *refs[XS - 1 :])


def theirs_kernel(*refs):
    parts, (keep, other, _, theirs) = refs[:XS], refs[XS:]
    for _, h, _, state in looked_after(parts, range(XS), keep, other):
        theirs[h] = state


def far_kernel(first, far, got, x_ref, gain_ref, _, out_ref):
    core, _ = place()
    mid = x_ref.shape[1] // 2
    for n in range(out_ref.shape[1] // 128):
        at = (first + n) * 128
        out_ref[:, n * 128 : n * 128 + 128] = finish_head(
            far, at, got[first + n], x_ref, (1 - core) * mid + at, gain_ref[...]
        )


def place_kernel(own, rest, far1, far2, out_hbm, sems):
    core, chip = place()
    mid = out_hbm.shape[1] // 2
    per = own.shape[1]

    def columns(at, size):
        return out_hbm.at[:, pl.ds(pl.multiple_of(at, 128), size)]

    there = (1 - core) * mid
    pairs = [(own, columns(core * mid + chip * per, per))]
    for shift in range(1, XS):
        part = rest.at[:, pl.ds((shift - 1) * per, per)]
        pairs.append((part, columns(core * mid + (chip + XS - shift) % XS * per, per)))
    pairs.append((far1, columns(there, far1.shape[1])))
    pairs.append((far2, columns(there + far1.shape[1], far2.shape[1])))
    for copy in fetch(pairs, sems):
        copy.wait()


def place_columns(width, *parts):
    return pl.pallas_call(
        place_kernel,
        in_specs=[VMEM] * len(parts),
        out_specs=pl.BlockSpec(memory_space=pltpu.HBM),
        out_shape=jax.ShapeDtypeStruct((parts[0].shape[0], width), BF16),
        scratch_shapes=[pltpu.SemaphoreType.DMA((XS + 2,))],
        compiler_params=pltpu.CompilerParams(vmem_limit_bytes=16 * 1024 * 1024),
        name="place_columns",
    )(*parts)


def swap_cores(array):
    return lax.ppermute(array, "ctx", [(i, i ^ 1) for i in range(lax.axis_size("ctx"))])


def along_x(array, shift):
    pairs = []
    for i in range(lax.axis_size("ctx")):
        row, chip, core = i // (2 * XS), i // 2 % XS, i % 2
        pairs.append((i, (row * XS + (chip + shift) % XS) * 2 + core))
    return lax.ppermute(array, "ctx", pairs)


def row_starts(keep, other):
    per = keep.shape[0] // XS
    parts = small_call(compose_kernel, [(per, 2, 128, 128)] * XS, (keep, other), "compose")
    parts = [parts[0]] + [along_x(parts[r], r) for r in range(1, XS)]
    ordered, total = small_call(
        total_kernel, [(XS, per, 2, 128, 128), (per, 128, 128)], parts, "row_total"
    )
    row = 2 * XS
    before = lax.ppermute(total, "ctx", [(i, i + row) for i in range(row)])
    starts = small_call(
        starts_kernel,
        [(per, 128, 128)] * XS,
        (ordered, before),
        "row_starts",
        [pltpu.VMEM((XS, per, 128, 128), BF16)],
    )
    return starts[0], [along_x(starts[r], r) for r in range(1, XS)]


def next_section(array):
    n = lax.axis_size("section")
    return lax.ppermute(array, "section", [(i, (i + 1) % n) for i in range(n)])


def on_device(layer_input, qk_weight, norm_gain, out_gain, log_decay, write_rate):
    keep, send, near, far, x = local_terms(
        layer_input[0], qk_weight[0], norm_gain, log_decay[0], write_rate[0]
    )
    other = swap_cores(send)
    own, rest = row_starts(keep, other)
    tokens, width = x.shape
    per = width // 2 // XS
    common = (keep, other, near, x, out_gain)
    done_own = small_call(near_own_kernel, [(tokens, per)], (own, *common), "finish_own")[0]
    done_own = next_section(done_own)
    done_rest = small_call(
        near_rest_kernel, [(tokens, (XS - 1) * per)], (*rest, *common), "finish_rest"
    )[0]
    done_rest = next_section(done_rest)
    theirs = small_call(
        theirs_kernel,
        [(keep.shape[0], 128, 128)],
        (own, *rest, keep, other, done_own),
        "other_core",
    )[0]
    got = swap_cores(theirs)

    def finish_far(first, after):
        done = small_call(
            functools.partial(far_kernel, first),
            [(tokens, width // 4)],
            (far, got, x, out_gain, after),
            "finish_far",
        )[0]
        return next_section(done)

    done_far1 = finish_far(0, done_own)
    done_far2 = finish_far(keep.shape[0] // 2, done_rest)
    return place_columns(width, done_own, done_rest, done_far1, done_far2)[None]


def solution(mesh):
    in_specs = (
        P("section", "ctx", None),
        P("section", None, None),
        P("section", None),
        P("section", None),
        P("section", None, "ctx"),
        P("section", None, "ctx"),
    )
    out_specs = P("section", "ctx", None)
    return jax.shard_map(
        on_device, mesh=mesh, in_specs=in_specs, out_specs=out_specs, check_vma=False
    )
```

```python
import functools

import jax
import jax.numpy as jnp
from jax import lax
from jax.experimental import pallas as pl
from jax.experimental.pallas import tpu as pltpu
from jax.sharding import PartitionSpec as P

F32 = jnp.float32
BF16 = jnp.bfloat16
EPS = 1e-6
HALF = 128
BASE = 8
GROUP = 8
XS = 4
VMEM = pl.BlockSpec(memory_space=pltpu.VMEM)


def in_hbm(array):
    return pltpu.with_memory_space_constraint(array, pltpu.HBM)


def place():
    at = lax.axis_index("ctx")
    return at % 2, at // 2 % XS


def mm(a, b):
    return jnp.dot(a, b, preferred_element_type=F32)


def iota(shape, dim):
    return lax.broadcasted_iota(jnp.int32, shape, dim)


def base_inverses(couplings):
    lanes = HALF
    count = len(couplings)
    blocks = lanes // BASE
    lane = iota((BASE, lanes), 1)
    packed = []
    for c in couplings:
        d = jnp.zeros((BASE, lanes), F32)
        for blk in range(blocks):
            d = jnp.where(lane // BASE == blk, c[blk * BASE : (blk + 1) * BASE, :], d)
        packed.append(d)
    d = jnp.concatenate(packed, axis=0)
    rows = count * BASE
    lane_all = iota((rows, lanes), 1)
    x = jnp.where(iota((rows, lanes), 0) % BASE == lane_all % BASE, 1.0, 0.0).astype(F32)
    x = x.reshape(count, BASE, lanes)
    for j in range(BASE - 1):
        spread = jnp.take_along_axis(d, lane_all // BASE * BASE + j, axis=1)
        x = x - spread.reshape(count, BASE, lanes) * x[:, j : j + 1, :]
    full = []
    for n in range(count):
        full.append(
            jnp.concatenate(
                [jnp.where(lane // BASE == blk, x[n], 0.0) for blk in range(blocks)], axis=0
            )
        )
    return full


def merge(inverses, couplings, m):
    kind = F32 if m < 16 else BF16
    size = HALF
    pairs = size // (2 * m)
    lane = iota((m, size), 1)
    odd_at = [(2 * p + 1) * m for p in range(pairs)]
    couplings = [c.astype(kind) for c in couplings]
    left = [
        jnp.concatenate(
            [
                jnp.where(lane // m == 2 * p, c[at : at + m, :], jnp.zeros((), kind))
                for p, at in enumerate(odd_at)
            ],
            axis=0,
        ).astype(BF16)
        for c in couplings
    ]
    middle = [mm(a, x.astype(BF16)).astype(kind) for a, x in zip(left, inverses)]
    blank = jnp.zeros((m, size), kind)
    spread = [
        jnp.concatenate(
            [part for p in range(pairs) for part in (blank, y[p * m : (p + 1) * m, :])], axis=0
        ).astype(BF16)
        for y in middle
    ]
    odd = [jnp.concatenate([x[at : at + m, :] for at in odd_at], axis=0) for x in inverses]
    lower = [mm(a.astype(BF16), y).astype(kind) for a, y in zip(odd, spread)]
    return [
        jnp.concatenate(
            [
                part
                for p, at in enumerate(odd_at)
                for part in (x[at - m : at, :], (o - z)[p * m : (p + 1) * m, :])
            ],
            axis=0,
        ).astype(BF16)
        for x, o, z in zip(inverses, odd, lower)
    ]


def split3(value):
    hi = value.astype(BF16)
    rest = value - hi.astype(F32)
    mid = rest.astype(BF16)
    return hi, mid, (rest - mid.astype(F32)).astype(BF16)


def fetch(pairs, sems):
    copies = [pltpu.make_async_copy(a, b, sems.at[n]) for n, (a, b) in enumerate(pairs)]
    for copy in copies:
        copy.start()
    return copies


def decays(n, cumul, cols):
    tokens = cols.shape[0]
    half = HALF
    incl = iota((half, half), 1) <= iota((half, half), 0)
    c = jnp.broadcast_to(cols[:, n : n + 1], (tokens, half))
    c_row = cumul[n : n + 1, :]
    c_mid = c_row[:, half - 1 : half]
    d00 = jnp.where(incl, jnp.exp(c[:half] - c_row[:, :half]), 0.0)
    d11 = jnp.where(incl, jnp.exp(c[half:] - c_row[:, half:]), 0.0)
    d10 = jnp.exp(c[half:] - c_mid) * jnp.exp(c_mid - c_row[:, :half])
    return c, c_row, d00, d10, d11


def group_pairs(s, normed, weight, cumul, cols, pairs_ref, unit_keys, solved_ref):
    tokens, width = normed.shape
    heads_all = cumul.shape[0]
    half = HALF
    core, _ = place()
    ri = iota((half, half), 0)
    ci = iota((half, half), 1)
    strict = ci < ri
    eye = ri == ci
    pk = mm(normed[...], weight)
    heads = []
    for h in range(GROUP):
        n = s * GROUP + h
        if h % 2 == 0:
            at = h // 2 * 128
            raw = pk[:, at : at + 128]
            k = (raw * lax.rsqrt(jnp.sum(raw * raw, axis=-1, keepdims=True) + EPS)).astype(BF16)
            unit_keys[:, at : at + 128] = k
            kt = k.T
            g0 = mm(k[:half], kt[:, :half])
            g1 = mm(k[half:], kt)
            kf = k.astype(F32)
            ktf = kt.astype(F32)
        c, c_row, d00, d10, d11 = decays(n, cumul, cols)
        b = jnp.broadcast_to(cols[:, heads_all + n : heads_all + n + 1], (tokens, half))
        c_end = c_row[:, tokens - 1 : tokens]
        l00 = jnp.where(strict, b[:half] * d00 * g0, 0.0)
        l11 = jnp.where(strict, b[half:] * d11 * g1[:, half:], 0.0)
        l10 = (b[half:] * d10 * g1[:, :half]).astype(BF16)
        v_at = pl.multiple_of((n * 128 + (1 - core) * (width // 2)) % width, 128)
        v = normed[:, pl.ds(v_at, 128)].astype(F32)
        right = jnp.concatenate([(b * v).astype(BF16), (b * jnp.exp(c) * kf).astype(BF16)], axis=1)
        carried_t = (ktf * jnp.exp(c_end - c_row)).astype(BF16)
        heads.append((l00, l11, l10, right, carried_t, jnp.exp(c_end)))

    inverses = base_inverses([c for hd in heads for c in hd[:2]])
    couplings = [c for hd in heads for c in hd[:2]]
    m = BASE
    while m < half:
        inverses = merge(inverses, couplings, m)
        m *= 2

    tops = [mm(x, hd[3][:half]).astype(BF16) for x, hd in zip(inverses[::2], heads)]
    rests = [
        (hd[3][half:].astype(F32) - mm(hd[2], top)).astype(BF16) for hd, top in zip(heads, tops)
    ]
    lows = [mm(x, rest).astype(BF16) for x, rest in zip(inverses[1::2], rests)]
    for h in range(GROUP):
        solved = jnp.concatenate([tops[h], lows[h]], axis=0)
        solved_ref[h] = solved
        pair = mm(heads[h][4], solved)
        pairs_ref[h, 0] = (jnp.where(eye, heads[h][5], 0.0) - pair[:, 128:]).astype(BF16)
        pairs_ref[h, 1] = pair[:, :128].astype(BF16)


def first_kernel(
    x_hbm, gain_hbm, decay_hbm, rate_hbm, w_hbm,
    pairs_ref, unit_keys, solved_ref, xbuf, normed, wk, wq, cumul_ref, cols_ref,
    gains, logs_buf, rates_buf, sems,
):
    tokens, width = xbuf.shape
    steps = wk.shape[0]
    wcols = wk.shape[2]
    heads_all = logs_buf.shape[0]
    mid_head = heads_all // 2
    core, _ = place()
    here = pl.multiple_of(core * mid_head, mid_head)
    there = pl.multiple_of((1 - core) * mid_head, mid_head)
    pairs = [(x_hbm, xbuf), (gain_hbm, gains)]
    for at, frm in ((0, there), (mid_head, here)):
        pairs.append((decay_hbm.at[pl.ds(frm, mid_head)], logs_buf.at[pl.ds(at, mid_head)]))
        pairs.append((rate_hbm.at[pl.ds(frm, mid_head)], rates_buf.at[pl.ds(at, mid_head)]))
    w_at = len(pairs)
    for base, to in ((width // 2, wk), (0, wq)):
        for s in range(steps):
            frm = (s * wcols + (1 - core) * (width // 4)) % (width // 2)
            frm = pl.multiple_of(base + frm, 128)
            pairs.append((w_hbm.at[:, pl.ds(frm, wcols)], to.at[s]))
    copies = fetch(pairs, sems)

    for copy in copies[2:w_at]:
        copy.wait()
    upto = (iota((tokens, tokens), 0) <= iota((tokens, tokens), 1)).astype(BF16)
    hi, mid, low = split3(logs_buf[...])
    cumul = mm(hi, upto) + (mm(mid, upto) + mm(low, upto))
    cols = jnp.concatenate([cumul, rates_buf[...]], axis=0).T
    cumul_ref[...] = cumul
    cols_ref[...] = cols

    copies[0].wait()
    copies[1].wait()
    for r in range(0, tokens, 64):
        xf = xbuf[r : r + 64, :].astype(F32)
        normed[r : r + 64, :] = (
            xf * lax.rsqrt(jnp.mean(xf * xf, axis=-1, keepdims=True) + EPS) * gains[...]
        ).astype(BF16)

    copies[w_at].wait()
    group_pairs(0, normed, wk[0], cumul, cols, pairs_ref, unit_keys, solved_ref)
    for copy in copies[w_at + 1 :]:
        copy.wait()


def last_kernel(normed, wk, cumul_ref, cols_ref, pairs_ref, unit_keys, solved_ref):
    group_pairs(
        1, normed, wk[1], cumul_ref[...], cols_ref[...], pairs_ref, unit_keys, solved_ref
    )


def group_shapes(x, heads):
    tokens, width = x.shape
    return [
        jax.ShapeDtypeStruct((GROUP, 2, 128, 128), BF16),
        jax.ShapeDtypeStruct((tokens, GROUP // 2 * 128), BF16),
        jax.ShapeDtypeStruct((GROUP, tokens, 256), BF16),
    ]


def pairs_call(kernel, in_specs, outs, scratch, name, args):
    return pl.pallas_call(
        kernel,
        in_specs=in_specs,
        out_specs=[VMEM] * len(outs),
        out_shape=outs,
        scratch_shapes=scratch,
        compiler_params=pltpu.CompilerParams(vmem_limit_bytes=24 * 1024 * 1024),
        cost_estimate=pl.CostEstimate(
            flops=5_000_000_000, bytes_accessed=8_000_000, transcendentals=1_000_000
        ),
        name=name,
    )(*args)


def first_pairs(x, weight, gain_in, log_decay, write_rate):
    tokens, width = x.shape
    heads = log_decay.shape[0]
    steps = heads // GROUP
    wcols = GROUP // 2 * 128
    weights = jax.ShapeDtypeStruct((steps, width, wcols), BF16)
    return pairs_call(
        first_kernel,
        [pl.BlockSpec(memory_space=pltpu.HBM)] * 5,
        group_shapes(x, heads)
        + [
            jax.ShapeDtypeStruct((tokens, width), BF16),
            jax.ShapeDtypeStruct((tokens, width), BF16),
            weights,
            weights,
            jax.ShapeDtypeStruct((heads, tokens), F32),
            jax.ShapeDtypeStruct((tokens, 2 * heads), F32),
        ],
        [
            pltpu.VMEM((1, width), F32),
            pltpu.VMEM((heads, tokens), F32),
            pltpu.VMEM((heads, tokens), F32),
            pltpu.SemaphoreType.DMA((6 + 2 * steps,)),
        ],
        "first_pairs",
        [in_hbm(a) for a in (x, gain_in, log_decay, write_rate, weight)],
    )


def last_pairs(normed, wk, cumul, cols):
    return pairs_call(
        last_kernel,
        [VMEM] * 4,
        group_shapes(normed, cumul.shape[0]),
        [],
        "last_pairs",
        (normed, wk, cumul, cols),
    )


def rows_kernel(s, normed, wq, unit_keys, solved_ref, cumul_ref, cols_ref, rows_ref):
    half = HALF
    tokens = normed.shape[0]
    pq = mm(normed[...], wq[s])
    cumul = cumul_ref[...]
    cols = cols_ref[...]
    heads = []
    for h in range(GROUP):
        n = s * GROUP + h
        if h % 2 == 0:
            at = h // 2 * 128
            q = pq[:, at : at + 128].astype(BF16)
            kt = unit_keys[:, at : at + 128].T
            g0 = mm(q[:half], kt[:, :half])
            g1 = mm(q[half:], kt)
            qf = q.astype(F32)
        c, _, d00, d10, d11 = decays(n, cumul, cols)
        s00 = (d00 * g0).astype(BF16)
        s1 = jnp.concatenate(
            [(d10 * g1[:, :half]).astype(BF16), (d11 * g1[:, half:]).astype(BF16)], axis=1
        )
        heads.append((s00, s1, jnp.exp(c) * qf))
    for h, (s00, s1, eq) in enumerate(heads):
        solved = solved_ref[h]
        out0 = mm(s00, solved[:half])
        out1 = mm(s1, solved)
        at = h * 128
        rows_ref[0, :half, at : at + 128] = (eq[:half] - out0[:, 128:]).astype(BF16)
        rows_ref[0, half:, at : at + 128] = (eq[half:] - out1[:, 128:]).astype(BF16)
        rows_ref[1, :half, at : at + 128] = out0[:, :128].astype(BF16)
        rows_ref[1, half:, at : at + 128] = out1[:, :128].astype(BF16)


def local_rows(s, *args):
    tokens = args[0].shape[0]
    return small_call(
        functools.partial(rows_kernel, s), [(2, tokens, GROUP * 128)], args, "local_rows"
    )[0]


def small_call(kernel, outs, args, name, scratch=()):
    return pl.pallas_call(
        kernel,
        in_specs=[VMEM] * len(args),
        out_specs=[VMEM] * len(outs),
        out_shape=[jax.ShapeDtypeStruct(shape, BF16) for shape in outs],
        scratch_shapes=list(scratch),
        compiler_params=pltpu.CompilerParams(vmem_limit_bytes=16 * 1024 * 1024),
        name=name,
    )(*args)


def compose_kernel(keep, other, *outs):
    core, chip = place()
    first = core == 0
    for shift, out in enumerate(outs):
        for i in range(out.shape[0]):
            h = (chip + shift) % XS * out.shape[0] + i
            mine, theirs = keep[h], other[h]
            early = jnp.where(first, mine, theirs)
            late = jnp.where(first, theirs, mine)
            prod = mm(late[0], jnp.concatenate([early[0], early[1]], axis=1))
            out[i, 0] = prod[:, :128].astype(BF16)
            out[i, 1] = (prod[:, 128:] + late[1].astype(F32)).astype(BF16)


def advance(trans, state, extra):
    hi = state.astype(BF16)
    low = (state - hi.astype(F32)).astype(BF16)
    prod = mm(trans, jnp.concatenate([hi, low], axis=1))
    return prod[:, :128] + prod[:, 128:] + extra.astype(F32)


def total_kernel(*refs):
    parts, (ordered, total) = refs[:XS], refs[XS:]
    _, chip = place()
    for shift, part in enumerate(parts):
        ordered[(chip + XS - shift) % XS] = part[...]
    for i in range(total.shape[0]):
        state = ordered[0, i, 1].astype(F32)
        for j in range(1, XS):
            state = advance(ordered[j, i, 0], state, ordered[j, i, 1])
        total[i] = state.astype(BF16)


def starts_kernel(ordered, before, _, *refs):
    outs, scratch = refs[:XS], refs[XS]
    _, chip = place()
    for i in range(before.shape[0]):
        state = before[i].astype(F32)
        for j in range(XS):
            scratch[(j + XS - chip) % XS, i] = state.astype(BF16)
            if j + 1 < XS:
                state = advance(ordered[j, i, 0], state, ordered[j, i, 1])
    for shift, out in enumerate(outs):
        out[...] = scratch[shift]


def finish_head(rows_ref, rows_at, state, x_ref, x_at, gain):
    cols = pl.ds(pl.multiple_of(rows_at, 128), 128)
    mixed = mm(rows_ref[0, :, cols], state) + rows_ref[1, :, cols].astype(F32)
    scaled = mixed * lax.rsqrt(jnp.mean(mixed * mixed, axis=-1, keepdims=True) + EPS) * gain
    rows = x_ref[:, pl.ds(pl.multiple_of(x_at, 128), 128)].astype(F32)
    return (rows + scaled.astype(BF16).astype(F32)).astype(BF16)


def looked_after(parts, shifts, keep, other):
    core, chip = place()
    first = core == 0
    at = 0
    for shift, part in zip(shifts, parts):
        for i in range(part.shape[0]):
            h = (chip + XS - shift) % XS * part.shape[0] + i
            early = jnp.where(first, keep[h], other[h])
            start = part[i]
            after = (mm(early[0], start) + early[1].astype(F32)).astype(BF16)
            yield at, h, jnp.where(first, start, after), jnp.where(first, after, start)
            at += 128


def near_heads(parts, shifts, keep, other, near, x_ref, gain_ref, out_ref):
    core, _ = place()
    mid = x_ref.shape[1] // 2
    for at, h, mine, _ in looked_after(parts, shifts, keep, other):
        out_ref[:, at : at + 128] = finish_head(
            near, h * 128, mine, x_ref, core * mid + h * 128, gain_ref[...]
        )


def near_own_kernel(part, *refs):
    near_heads([part], [0], *refs)


def near_rest_kernel(*refs):
    near_heads(refs[: XS - 1], range(1, XS), *refs[XS - 1 :])


def theirs_kernel(*refs):
    parts, (keep, other, _, theirs) = refs[:XS], refs[XS:]
    for _, h, _, state in looked_after(parts, range(XS), keep, other):
        theirs[h] = state


def far_kernel(first, far, got, x_ref, gain_ref, _, out_ref):
    core, _ = place()
    mid = x_ref.shape[1] // 2
    for n in range(out_ref.shape[1] // 128):
        at = (first + n) * 128
        out_ref[:, n * 128 : n * 128 + 128] = finish_head(
            far, at, got[first + n], x_ref, (1 - core) * mid + at, gain_ref[...]
        )


def place_kernel(own, rest, far1, far2, out_hbm, sems):
    core, chip = place()
    mid = out_hbm.shape[1] // 2
    per = own.shape[1]

    def columns(at, size):
        return out_hbm.at[:, pl.ds(pl.multiple_of(at, 128), size)]

    there = (1 - core) * mid
    pairs = [(own, columns(core * mid + chip * per, per))]
    for shift in range(1, XS):
        part = rest.at[:, pl.ds((shift - 1) * per, per)]
        pairs.append((part, columns(core * mid + (chip + XS - shift) % XS * per, per)))
    pairs.append((far1, columns(there, far1.shape[1])))
    pairs.append((far2, columns(there + far1.shape[1], far2.shape[1])))
    for copy in fetch(pairs, sems):
        copy.wait()


def place_columns(width, *parts):
    return pl.pallas_call(
        place_kernel,
        in_specs=[VMEM] * len(parts),
        out_specs=pl.BlockSpec(memory_space=pltpu.HBM),
        out_shape=jax.ShapeDtypeStruct((parts[0].shape[0], width), BF16),
        scratch_shapes=[pltpu.SemaphoreType.DMA((XS + 2,))],
        compiler_params=pltpu.CompilerParams(vmem_limit_bytes=16 * 1024 * 1024),
        name="place_columns",
    )(*parts)


def swap_cores(array):
    return lax.ppermute(array, "ctx", [(i, i ^ 1) for i in range(lax.axis_size("ctx"))])


def along_x(array, shift):
    pairs = []
    for i in range(lax.axis_size("ctx")):
        row, chip, core = i // (2 * XS), i // 2 % XS, i % 2
        pairs.append((i, (row * XS + (chip + shift) % XS) * 2 + core))
    return lax.ppermute(array, "ctx", pairs)


def row_starts(keep, other, near):
    per = keep.shape[0] // XS
    parts = small_call(compose_kernel, [(per, 2, 128, 128)] * XS, (keep, other), "compose")
    parts = [parts[0]] + [along_x(parts[r], r) for r in range(1, XS)]
    ordered, total = small_call(
        total_kernel, [(XS, per, 2, 128, 128), (per, 128, 128)], parts, "row_total"
    )
    row = 2 * XS
    before = lax.ppermute(total, "ctx", [(i, i + row) for i in range(row)])
    starts = small_call(
        starts_kernel,
        [(per, 128, 128)] * XS,
        (ordered, before, near),
        "row_starts",
        [pltpu.VMEM((XS, per, 128, 128), BF16)],
    )
    return starts[0], [along_x(starts[r], r) for r in range(1, XS)]


def next_section(array):
    n = lax.axis_size("section")
    return lax.ppermute(array, "section", [(i, (i + 1) % n) for i in range(n)])


def on_device(layer_input, qk_weight, norm_gain, out_gain, log_decay, write_rate):
    send, far_keys, far_solved, x, normed, wk, wq, cumul, cols = first_pairs(
        layer_input[0], qk_weight[0], norm_gain, log_decay[0], write_rate[0]
    )
    other = swap_cores(send)
    keep, near_keys, near_solved = last_pairs(normed, wk, cumul, cols)
    near = local_rows(1, normed, wq, near_keys, near_solved, cumul, cols)
    far = local_rows(0, normed, wq, far_keys, far_solved, cumul, cols)
    own, rest = row_starts(keep, other, near)
    tokens, width = x.shape
    per = width // 2 // XS
    common = (keep, other, near, x, out_gain)
    done_own = small_call(near_own_kernel, [(tokens, per)], (own, *common), "finish_own")[0]
    done_own = next_section(done_own)
    done_rest = small_call(
        near_rest_kernel, [(tokens, (XS - 1) * per)], (*rest, *common), "finish_rest"
    )[0]
    done_rest = next_section(done_rest)
    theirs = small_call(
        theirs_kernel,
        [(keep.shape[0], 128, 128)],
        (own, *rest, keep, other, done_own),
        "other_core",
    )[0]
    got = swap_cores(theirs)

    def finish_far(first, after):
        done = small_call(
            functools.partial(far_kernel, first),
            [(tokens, width // 4)],
            (far, got, x, out_gain, after),
            "finish_far",
        )[0]
        return next_section(done)

    done_far1 = finish_far(0, done_own)
    done_far2 = finish_far(keep.shape[0] // 2, done_rest)
    return place_columns(width, done_own, done_rest, done_far1, done_far2)[None]


def solution(mesh):
    in_specs = (
        P("section", "ctx", None),
        P("section", None, None),
        P("section", None),
        P("section", None),
        P("section", None, "ctx"),
        P("section", None, "ctx"),
    )
    out_specs = P("section", "ctx", None)
    return jax.shard_map(
        on_device, mesh=mesh, in_specs=in_specs, out_specs=out_specs, check_vma=False
    )
```

```python
import functools

import jax
import jax.numpy as jnp
from jax import lax
from jax.experimental import pallas as pl
from jax.experimental.pallas import tpu as pltpu
from jax.sharding import PartitionSpec as P

F32 = jnp.float32
BF16 = jnp.bfloat16
EPS = 1e-6
HALF = 128
BASE = 8
GROUP = 8
XS = 4
SPLIT = 4
VMEM = pl.BlockSpec(memory_space=pltpu.VMEM)


def in_hbm(array):
    return pltpu.with_memory_space_constraint(array, pltpu.HBM)


def place():
    at = lax.axis_index("ctx")
    return at % 2, at // 2 % XS


def mm(a, b):
    return jnp.dot(a, b, preferred_element_type=F32)


def iota(shape, dim):
    return lax.broadcasted_iota(jnp.int32, shape, dim)


def base_inverses(couplings):
    lanes = HALF
    count = len(couplings)
    blocks = lanes // BASE
    lane = iota((BASE, lanes), 1)
    packed = []
    for c in couplings:
        d = jnp.zeros((BASE, lanes), F32)
        for blk in range(blocks):
            d = jnp.where(lane // BASE == blk, c[blk * BASE : (blk + 1) * BASE, :], d)
        packed.append(d)
    d = jnp.concatenate(packed, axis=0)
    rows = count * BASE
    lane_all = iota((rows, lanes), 1)
    x = jnp.where(iota((rows, lanes), 0) % BASE == lane_all % BASE, 1.0, 0.0).astype(F32)
    x = x.reshape(count, BASE, lanes)
    for j in range(BASE - 1):
        spread = jnp.take_along_axis(d, lane_all // BASE * BASE + j, axis=1)
        x = x - spread.reshape(count, BASE, lanes) * x[:, j : j + 1, :]
    full = []
    for n in range(count):
        full.append(
            jnp.concatenate(
                [jnp.where(lane // BASE == blk, x[n], 0.0) for blk in range(blocks)], axis=0
            )
        )
    return full


def merge(inverses, couplings, m):
    kind = F32 if m < 16 else BF16
    size = HALF
    pairs = size // (2 * m)
    lane = iota((m, size), 1)
    odd_at = [(2 * p + 1) * m for p in range(pairs)]
    couplings = [c.astype(kind) for c in couplings]
    left = [
        jnp.concatenate(
            [
                jnp.where(lane // m == 2 * p, c[at : at + m, :], jnp.zeros((), kind))
                for p, at in enumerate(odd_at)
            ],
            axis=0,
        ).astype(BF16)
        for c in couplings
    ]
    middle = [mm(a, x.astype(BF16)).astype(kind) for a, x in zip(left, inverses)]
    blank = jnp.zeros((m, size), kind)
    spread = [
        jnp.concatenate(
            [part for p in range(pairs) for part in (blank, y[p * m : (p + 1) * m, :])], axis=0
        ).astype(BF16)
        for y in middle
    ]
    odd = [jnp.concatenate([x[at : at + m, :] for at in odd_at], axis=0) for x in inverses]
    lower = [mm(a.astype(BF16), y).astype(kind) for a, y in zip(odd, spread)]
    return [
        jnp.concatenate(
            [
                part
                for p, at in enumerate(odd_at)
                for part in (x[at - m : at, :], (o - z)[p * m : (p + 1) * m, :])
            ],
            axis=0,
        ).astype(BF16)
        for x, o, z in zip(inverses, odd, lower)
    ]


def split3(value):
    hi = value.astype(BF16)
    rest = value - hi.astype(F32)
    mid = rest.astype(BF16)
    return hi, mid, (rest - mid.astype(F32)).astype(BF16)


def fetch(pairs, sems):
    copies = [pltpu.make_async_copy(a, b, sems.at[n]) for n, (a, b) in enumerate(pairs)]
    for copy in copies:
        copy.start()
    return copies


def decays(n, cumul, cols):
    tokens = cols.shape[0]
    half = HALF
    incl = iota((half, half), 1) <= iota((half, half), 0)
    c = jnp.broadcast_to(cols[:, n : n + 1], (tokens, half))
    c_row = cumul[n : n + 1, :]
    c_mid = c_row[:, half - 1 : half]
    d00 = jnp.where(incl, jnp.exp(c[:half] - c_row[:, :half]), 0.0)
    d11 = jnp.where(incl, jnp.exp(c[half:] - c_row[:, half:]), 0.0)
    d10 = jnp.exp(c[half:] - c_mid) * jnp.exp(c_mid - c_row[:, :half])
    return c, c_row, d00, d10, d11


def group_pairs(s, normed, weight, cumul, cols, pairs_ref, unit_keys, solved_ref):
    tokens, width = normed.shape
    heads_all = cumul.shape[0]
    half = HALF
    core, _ = place()
    ri = iota((half, half), 0)
    ci = iota((half, half), 1)
    strict = ci < ri
    eye = ri == ci
    pk = mm(normed[...], weight)
    heads = []
    for h in range(GROUP):
        n = s * GROUP + h
        if h % 2 == 0:
            at = h // 2 * 128
            raw = pk[:, at : at + 128]
            k = (raw * lax.rsqrt(jnp.sum(raw * raw, axis=-1, keepdims=True) + EPS)).astype(BF16)
            unit_keys[:, at : at + 128] = k
            kt = k.T
            g0 = mm(k[:half], kt[:, :half])
            g1 = mm(k[half:], kt)
            kf = k.astype(F32)
            ktf = kt.astype(F32)
        c, c_row, d00, d10, d11 = decays(n, cumul, cols)
        b = jnp.broadcast_to(cols[:, heads_all + n : heads_all + n + 1], (tokens, half))
        c_end = c_row[:, tokens - 1 : tokens]
        l00 = jnp.where(strict, b[:half] * d00 * g0, 0.0)
        l11 = jnp.where(strict, b[half:] * d11 * g1[:, half:], 0.0)
        l10 = (b[half:] * d10 * g1[:, :half]).astype(BF16)
        v_at = pl.multiple_of((n * 128 + (1 - core) * (width // 2)) % width, 128)
        v = normed[:, pl.ds(v_at, 128)].astype(F32)
        right = jnp.concatenate([(b * v).astype(BF16), (b * jnp.exp(c) * kf).astype(BF16)], axis=1)
        carried_t = (ktf * jnp.exp(c_end - c_row)).astype(BF16)
        heads.append((l00, l11, l10, right, carried_t, jnp.exp(c_end)))

    inverses = base_inverses([c for hd in heads for c in hd[:2]])
    couplings = [c for hd in heads for c in hd[:2]]
    m = BASE
    while m < half:
        inverses = merge(inverses, couplings, m)
        m *= 2

    tops = [mm(x, hd[3][:half]).astype(BF16) for x, hd in zip(inverses[::2], heads)]
    rests = [
        (hd[3][half:].astype(F32) - mm(hd[2], top)).astype(BF16) for hd, top in zip(heads, tops)
    ]
    lows = [mm(x, rest).astype(BF16) for x, rest in zip(inverses[1::2], rests)]
    for h in range(GROUP):
        solved = jnp.concatenate([tops[h], lows[h]], axis=0)
        solved_ref[h] = solved
        pair = mm(heads[h][4], solved)
        pairs_ref[h, 0] = (jnp.where(eye, heads[h][5], 0.0) - pair[:, 128:]).astype(BF16)
        pairs_ref[h, 1] = pair[:, :128].astype(BF16)


def first_kernel(
    x_hbm, gain_hbm, decay_hbm, rate_hbm, w_hbm,
    pairs_ref, unit_keys, solved_ref, xbuf, normed, wk, wq, cumul_ref, cols_ref,
    gains, logs_buf, rates_buf, sems,
):
    tokens, width = xbuf.shape
    steps = wk.shape[0]
    wcols = wk.shape[2]
    heads_all = logs_buf.shape[0]
    mid_head = heads_all // 2
    core, _ = place()
    here = pl.multiple_of(core * mid_head, mid_head)
    there = pl.multiple_of((1 - core) * mid_head, mid_head)
    pairs = [(gain_hbm, gains)]
    for at, frm in ((0, there), (mid_head, here)):
        pairs.append((decay_hbm.at[pl.ds(frm, mid_head)], logs_buf.at[pl.ds(at, mid_head)]))
        pairs.append((rate_hbm.at[pl.ds(frm, mid_head)], rates_buf.at[pl.ds(at, mid_head)]))
    x_at = len(pairs)
    rows = tokens // SPLIT
    for r in range(0, tokens, rows):
        pairs.append((x_hbm.at[pl.ds(r, rows)], xbuf.at[pl.ds(r, rows)]))
    w_at = len(pairs)
    rows = width // SPLIT
    for base, to in ((width // 2, wk), (0, wq)):
        for s in range(steps):
            frm = (s * wcols + (1 - core) * (width // 4)) % (width // 2)
            frm = pl.multiple_of(base + frm, 128)
            for r in range(0, width, rows):
                part = w_hbm.at[pl.ds(r, rows), pl.ds(frm, wcols)]
                pairs.append((part, to.at[s, pl.ds(r, rows)]))
    copies = fetch(pairs, sems)

    for copy in copies[:x_at]:
        copy.wait()
    upto = (iota((tokens, tokens), 0) <= iota((tokens, tokens), 1)).astype(BF16)
    hi, mid, low = split3(logs_buf[...])
    cumul = mm(hi, upto) + (mm(mid, upto) + mm(low, upto))
    cols = jnp.concatenate([cumul, rates_buf[...]], axis=0).T
    cumul_ref[...] = cumul
    cols_ref[...] = cols

    rows = tokens // SPLIT
    for n, r in enumerate(range(0, tokens, rows)):
        copies[x_at + n].wait()
        xf = xbuf[r : r + rows, :].astype(F32)
        normed[r : r + rows, :] = (
            xf * lax.rsqrt(jnp.mean(xf * xf, axis=-1, keepdims=True) + EPS) * gains[...]
        ).astype(BF16)

    for copy in copies[w_at : w_at + SPLIT]:
        copy.wait()
    group_pairs(0, normed, wk[0], cumul, cols, pairs_ref, unit_keys, solved_ref)
    for copy in copies[w_at + SPLIT :]:
        copy.wait()


def last_kernel(normed, wk, cumul_ref, cols_ref, pairs_ref, unit_keys, solved_ref):
    group_pairs(
        1, normed, wk[1], cumul_ref[...], cols_ref[...], pairs_ref, unit_keys, solved_ref
    )


def group_shapes(x, heads):
    tokens, width = x.shape
    return [
        jax.ShapeDtypeStruct((GROUP, 2, 128, 128), BF16),
        jax.ShapeDtypeStruct((tokens, GROUP // 2 * 128), BF16),
        jax.ShapeDtypeStruct((GROUP, tokens, 256), BF16),
    ]


def pairs_call(kernel, in_specs, outs, scratch, name, args):
    return pl.pallas_call(
        kernel,
        in_specs=in_specs,
        out_specs=[VMEM] * len(outs),
        out_shape=outs,
        scratch_shapes=scratch,
        compiler_params=pltpu.CompilerParams(vmem_limit_bytes=24 * 1024 * 1024),
        cost_estimate=pl.CostEstimate(
            flops=5_000_000_000, bytes_accessed=8_000_000, transcendentals=1_000_000
        ),
        name=name,
    )(*args)


def first_pairs(x, weight, gain_in, log_decay, write_rate):
    tokens, width = x.shape
    heads = log_decay.shape[0]
    steps = heads // GROUP
    wcols = GROUP // 2 * 128
    weights = jax.ShapeDtypeStruct((steps, width, wcols), BF16)
    return pairs_call(
        first_kernel,
        [pl.BlockSpec(memory_space=pltpu.HBM)] * 5,
        group_shapes(x, heads)
        + [
            jax.ShapeDtypeStruct((tokens, width), BF16),
            jax.ShapeDtypeStruct((tokens, width), BF16),
            weights,
            weights,
            jax.ShapeDtypeStruct((heads, tokens), F32),
            jax.ShapeDtypeStruct((tokens, 2 * heads), F32),
        ],
        [
            pltpu.VMEM((1, width), F32),
            pltpu.VMEM((heads, tokens), F32),
            pltpu.VMEM((heads, tokens), F32),
            pltpu.SemaphoreType.DMA((5 + (1 + 2 * steps) * SPLIT,)),
        ],
        "first_pairs",
        [in_hbm(a) for a in (x, gain_in, log_decay, write_rate, weight)],
    )


def last_pairs(normed, wk, cumul, cols):
    return pairs_call(
        last_kernel,
        [VMEM] * 4,
        group_shapes(normed, cumul.shape[0]),
        [],
        "last_pairs",
        (normed, wk, cumul, cols),
    )


def rows_kernel(s, normed, wq, unit_keys, solved_ref, cumul_ref, cols_ref, rows_ref):
    half = HALF
    tokens = normed.shape[0]
    pq = mm(normed[...], wq[s])
    cumul = cumul_ref[...]
    cols = cols_ref[...]
    heads = []
    for h in range(GROUP):
        n = s * GROUP + h
        if h % 2 == 0:
            at = h // 2 * 128
            q = pq[:, at : at + 128].astype(BF16)
            kt = unit_keys[:, at : at + 128].T
            g0 = mm(q[:half], kt[:, :half])
            g1 = mm(q[half:], kt)
            qf = q.astype(F32)
        c, _, d00, d10, d11 = decays(n, cumul, cols)
        s00 = (d00 * g0).astype(BF16)
        s1 = jnp.concatenate(
            [(d10 * g1[:, :half]).astype(BF16), (d11 * g1[:, half:]).astype(BF16)], axis=1
        )
        heads.append((s00, s1, jnp.exp(c) * qf))
    for h, (s00, s1, eq) in enumerate(heads):
        solved = solved_ref[h]
        out0 = mm(s00, solved[:half])
        out1 = mm(s1, solved)
        at = h * 128
        rows_ref[0, :half, at : at + 128] = (eq[:half] - out0[:, 128:]).astype(BF16)
        rows_ref[0, half:, at : at + 128] = (eq[half:] - out1[:, 128:]).astype(BF16)
        rows_ref[1, :half, at : at + 128] = out0[:, :128].astype(BF16)
        rows_ref[1, half:, at : at + 128] = out1[:, :128].astype(BF16)


def local_rows(s, *args):
    tokens = args[0].shape[0]
    return small_call(
        functools.partial(rows_kernel, s), [(2, tokens, GROUP * 128)], args, "local_rows"
    )[0]


def small_call(kernel, outs, args, name, scratch=()):
    return pl.pallas_call(
        kernel,
        in_specs=[VMEM] * len(args),
        out_specs=[VMEM] * len(outs),
        out_shape=[jax.ShapeDtypeStruct(shape, BF16) for shape in outs],
        scratch_shapes=list(scratch),
        compiler_params=pltpu.CompilerParams(vmem_limit_bytes=16 * 1024 * 1024),
        name=name,
    )(*args)


def compose_kernel(keep, other, *outs):
    core, chip = place()
    first = core == 0
    for shift, out in enumerate(outs):
        for i in range(out.shape[0]):
            h = (chip + shift) % XS * out.shape[0] + i
            mine, theirs = keep[h], other[h]
            early = jnp.where(first, mine, theirs)
            late = jnp.where(first, theirs, mine)
            prod = mm(late[0], jnp.concatenate([early[0], early[1]], axis=1))
            out[i, 0] = prod[:, :128].astype(BF16)
            out[i, 1] = (prod[:, 128:] + late[1].astype(F32)).astype(BF16)


def advance(pairs, states):
    his = [state.astype(BF16) for state in states]
    both = [
        jnp.concatenate([hi, (state - hi.astype(F32)).astype(BF16)], axis=1)
        for hi, state in zip(his, states)
    ]
    prods = [mm(pair[0], b) for pair, b in zip(pairs, both)]
    return [
        prod[:, :128] + prod[:, 128:] + pair[1].astype(F32) for pair, prod in zip(pairs, prods)
    ]


def total_kernel(*refs):
    parts, (ordered, total) = refs[:XS], refs[XS:]
    _, chip = place()
    for shift, part in enumerate(parts):
        ordered[(chip + XS - shift) % XS] = part[...]
    per = total.shape[0]
    states = [ordered[0, i, 1].astype(F32) for i in range(per)]
    for j in range(1, XS):
        states = advance([ordered[j, i] for i in range(per)], states)
    for i in range(per):
        total[i] = states[i].astype(BF16)


def starts_kernel(ordered, before, _, *refs):
    outs, scratch = refs[:XS], refs[XS]
    _, chip = place()
    per = before.shape[0]
    states = [before[i].astype(F32) for i in range(per)]
    for j in range(XS):
        for i in range(per):
            scratch[(j + XS - chip) % XS, i] = states[i].astype(BF16)
        if j + 1 < XS:
            states = advance([ordered[j, i] for i in range(per)], states)
    for shift, out in enumerate(outs):
        out[...] = scratch[shift]


def finish_heads(rows_ref, rows_at, states, x_ref, x_at, gain, out_ref):
    where = [pl.ds(pl.multiple_of(at, 128), 128) for at in rows_at]
    mixed = [mm(rows_ref[0, :, w], state) for w, state in zip(where, states)]
    mixed = [m + rows_ref[1, :, w].astype(F32) for m, w in zip(mixed, where)]
    scales = [lax.rsqrt(jnp.mean(m * m, axis=-1, keepdims=True) + EPS) for m in mixed]
    for n, (m, scale, at) in enumerate(zip(mixed, scales, x_at)):
        rows = x_ref[:, pl.ds(pl.multiple_of(at, 128), 128)].astype(F32)
        branch = (m * scale * gain).astype(BF16).astype(F32)
        out_ref[:, n * 128 : n * 128 + 128] = (rows + branch).astype(BF16)


def looked_after(parts, shifts, keep, other):
    core, chip = place()
    first = core == 0
    heads, starts = [], []
    for shift, part in zip(shifts, parts):
        for i in range(part.shape[0]):
            heads.append((chip + XS - shift) % XS * part.shape[0] + i)
            starts.append(part[i])
    early = [jnp.where(first, keep[h], other[h]) for h in heads]
    after = [mm(e[0], start) for e, start in zip(early, starts)]
    after = [(a + e[1].astype(F32)).astype(BF16) for a, e in zip(after, early)]
    mine = [jnp.where(first, a, b) for a, b in zip(starts, after)]
    theirs = [jnp.where(first, b, a) for a, b in zip(starts, after)]
    return heads, mine, theirs


def near_heads(parts, shifts, keep, other, near, x_ref, gain_ref, out_ref):
    core, _ = place()
    mid = x_ref.shape[1] // 2
    heads, mine, _ = looked_after(parts, shifts, keep, other)
    rows_at = [h * 128 for h in heads]
    x_at = [core * mid + h * 128 for h in heads]
    finish_heads(near, rows_at, mine, x_ref, x_at, gain_ref[...], out_ref)


def near_own_kernel(part, *refs):
    near_heads([part], [0], *refs)


def near_rest_kernel(*refs):
    near_heads(refs[: XS - 1], range(1, XS), *refs[XS - 1 :])


def theirs_kernel(*refs):
    parts, (keep, other, _, theirs) = refs[:XS], refs[XS:]
    heads, _, states = looked_after(parts, range(XS), keep, other)
    for h, state in zip(heads, states):
        theirs[h] = state


def far_kernel(first, far, got, x_ref, gain_ref, _, out_ref):
    core, _ = place()
    mid = x_ref.shape[1] // 2
    heads = range(first, first + out_ref.shape[1] // 128)
    rows_at = [h * 128 for h in heads]
    x_at = [(1 - core) * mid + at for at in rows_at]
    finish_heads(far, rows_at, [got[h] for h in heads], x_ref, x_at, gain_ref[...], out_ref)


def place_kernel(own, rest, far1, out_hbm, sems):
    core, chip = place()
    mid = out_hbm.shape[1] // 2
    per = own.shape[1]

    def columns(at, size):
        return out_hbm.at[:, pl.ds(pl.multiple_of(at, 128), size)]

    pairs = [(own, columns(core * mid + chip * per, per))]
    for shift in range(1, XS):
        part = rest.at[:, pl.ds((shift - 1) * per, per)]
        pairs.append((part, columns(core * mid + (chip + XS - shift) % XS * per, per)))
    pairs.append((far1, columns((1 - core) * mid, far1.shape[1])))
    for copy in fetch(pairs, sems):
        copy.wait()


def place_last_kernel(far2, _, out_hbm, sems):
    core, _ = place()
    cols = far2.shape[1]
    at = pl.multiple_of((1 - core) * 2 * cols + cols, 128)
    for copy in fetch([(far2, out_hbm.at[:, pl.ds(at, cols)])], sems):
        copy.wait()


def place_columns(width, kernel, parts, name, out=None):
    hbm = pl.BlockSpec(memory_space=pltpu.HBM)
    last = () if out is None else (out,)
    return pl.pallas_call(
        kernel,
        in_specs=[VMEM] * len(parts) + [hbm] * len(last),
        out_specs=hbm,
        out_shape=jax.ShapeDtypeStruct((parts[0].shape[0], width), BF16),
        scratch_shapes=[pltpu.SemaphoreType.DMA((XS + 1,))],
        input_output_aliases={len(parts): 0} if last else {},
        compiler_params=pltpu.CompilerParams(vmem_limit_bytes=16 * 1024 * 1024),
        name=name,
    )(*parts, *last)


def swap_cores(array):
    return lax.ppermute(array, "ctx", [(i, i ^ 1) for i in range(lax.axis_size("ctx"))])


def along_x(array, shift):
    pairs = []
    for i in range(lax.axis_size("ctx")):
        row, chip, core = i // (2 * XS), i // 2 % XS, i % 2
        pairs.append((i, (row * XS + (chip + shift) % XS) * 2 + core))
    return lax.ppermute(array, "ctx", pairs)


def row_starts(keep, other, near):
    per = keep.shape[0] // XS
    parts = small_call(compose_kernel, [(per, 2, 128, 128)] * XS, (keep, other), "compose")
    parts = [parts[0]] + [along_x(parts[r], r) for r in range(1, XS)]
    ordered, total = small_call(
        total_kernel, [(XS, per, 2, 128, 128), (per, 128, 128)], parts, "row_total"
    )
    row = 2 * XS
    before = lax.ppermute(total, "ctx", [(i, i + row) for i in range(row)])
    starts = small_call(
        starts_kernel,
        [(per, 128, 128)] * XS,
        (ordered, before, near),
        "row_starts",
        [pltpu.VMEM((XS, per, 128, 128), BF16)],
    )
    return starts[0], [along_x(starts[r], r) for r in range(1, XS)]


def next_section(array):
    n = lax.axis_size("section")
    return lax.ppermute(array, "section", [(i, (i + 1) % n) for i in range(n)])


def on_device(layer_input, qk_weight, norm_gain, out_gain, log_decay, write_rate):
    send, far_keys, far_solved, x, normed, wk, wq, cumul, cols = first_pairs(
        layer_input[0], qk_weight[0], norm_gain, log_decay[0], write_rate[0]
    )
    other = swap_cores(send)
    keep, near_keys, near_solved = last_pairs(normed, wk, cumul, cols)
    near = local_rows(1, normed, wq, near_keys, near_solved, cumul, cols)
    far = local_rows(0, normed, wq, far_keys, far_solved, cumul, cols)
    own, rest = row_starts(keep, other, near)
    tokens, width = x.shape
    per = width // 2 // XS
    common = (keep, other, near, x, out_gain)
    done_own = small_call(near_own_kernel, [(tokens, per)], (own, *common), "finish_own")[0]
    done_own = next_section(done_own)
    done_rest = small_call(
        near_rest_kernel, [(tokens, (XS - 1) * per)], (*rest, *common), "finish_rest"
    )[0]
    done_rest = next_section(done_rest)
    theirs = small_call(
        theirs_kernel,
        [(keep.shape[0], 128, 128)],
        (own, *rest, keep, other, done_own),
        "other_core",
    )[0]
    got = swap_cores(theirs)

    def finish_far(first, after):
        done = small_call(
            functools.partial(far_kernel, first),
            [(tokens, width // 4)],
            (far, got, x, out_gain, after),
            "finish_far",
        )[0]
        return next_section(done)

    done_far1 = finish_far(0, done_own)
    done_far2 = finish_far(keep.shape[0] // 2, done_rest)
    most = place_columns(width, place_kernel, (done_own, done_rest, done_far1), "place_most")
    return place_columns(width, place_last_kernel, (done_far2,), "place_last", most)[None]


def solution(mesh):
    in_specs = (
        P("section", "ctx", None),
        P("section", None, None),
        P("section", None),
        P("section", None),
        P("section", None, "ctx"),
        P("section", None, "ctx"),
    )
    out_specs = P("section", "ctx", None)
    return jax.shard_map(
        on_device, mesh=mesh, in_specs=in_specs, out_specs=out_specs, check_vma=False
    )
```

```python
import functools

import jax
import jax.numpy as jnp
from jax import lax
from jax.experimental import pallas as pl
from jax.experimental.pallas import tpu as pltpu
from jax.sharding import PartitionSpec as P

F32 = jnp.float32
BF16 = jnp.bfloat16
EPS = 1e-6
HALF = 128
BASE = 8
GROUP = 8
XS = 4
SPLIT = 4
VMEM = pl.BlockSpec(memory_space=pltpu.VMEM)


def in_hbm(array):
    return pltpu.with_memory_space_constraint(array, pltpu.HBM)


def place():
    at = lax.axis_index("ctx")
    return at % 2, at // 2 % XS


def mm(a, b):
    return jnp.dot(a, b, preferred_element_type=F32)


def iota(shape, dim):
    return lax.broadcasted_iota(jnp.int32, shape, dim)


def base_inverses(couplings):
    lanes = HALF
    count = len(couplings)
    blocks = lanes // BASE
    lane = iota((BASE, lanes), 1)
    packed = []
    for c in couplings:
        d = jnp.zeros((BASE, lanes), F32)
        for blk in range(blocks):
            d = jnp.where(lane // BASE == blk, c[blk * BASE : (blk + 1) * BASE, :], d)
        packed.append(d)
    d = jnp.concatenate(packed, axis=0)
    rows = count * BASE
    lane_all = iota((rows, lanes), 1)
    x = jnp.where(iota((rows, lanes), 0) % BASE == lane_all % BASE, 1.0, 0.0).astype(F32)
    x = x.reshape(count, BASE, lanes)
    for j in range(BASE - 1):
        spread = jnp.take_along_axis(d, lane_all // BASE * BASE + j, axis=1)
        x = x - spread.reshape(count, BASE, lanes) * x[:, j : j + 1, :]
    full = []
    for n in range(count):
        full.append(
            jnp.concatenate(
                [jnp.where(lane // BASE == blk, x[n], 0.0) for blk in range(blocks)], axis=0
            )
        )
    return full


def merge(inverses, couplings, m):
    kind = F32 if m < 16 else BF16
    size = HALF
    pairs = size // (2 * m)
    lane = iota((m, size), 1)
    odd_at = [(2 * p + 1) * m for p in range(pairs)]
    couplings = [c.astype(kind) for c in couplings]
    left = [
        jnp.concatenate(
            [
                jnp.where(lane // m == 2 * p, c[at : at + m, :], jnp.zeros((), kind))
                for p, at in enumerate(odd_at)
            ],
            axis=0,
        ).astype(BF16)
        for c in couplings
    ]
    middle = [mm(a, x.astype(BF16)).astype(kind) for a, x in zip(left, inverses)]
    blank = jnp.zeros((m, size), kind)
    spread = [
        jnp.concatenate(
            [part for p in range(pairs) for part in (blank, y[p * m : (p + 1) * m, :])], axis=0
        ).astype(BF16)
        for y in middle
    ]
    odd = [jnp.concatenate([x[at : at + m, :] for at in odd_at], axis=0) for x in inverses]
    lower = [mm(a.astype(BF16), y).astype(kind) for a, y in zip(odd, spread)]
    return [
        jnp.concatenate(
            [
                part
                for p, at in enumerate(odd_at)
                for part in (x[at - m : at, :], (o - z)[p * m : (p + 1) * m, :])
            ],
            axis=0,
        ).astype(BF16)
        for x, o, z in zip(inverses, odd, lower)
    ]


def split3(value):
    hi = value.astype(BF16)
    rest = value - hi.astype(F32)
    mid = rest.astype(BF16)
    return hi, mid, (rest - mid.astype(F32)).astype(BF16)


def fetch(pairs, sems):
    copies = [pltpu.make_async_copy(a, b, sems.at[n]) for n, (a, b) in enumerate(pairs)]
    for copy in copies:
        copy.start()
    return copies


def decays(n, cumul, cols):
    tokens = cols.shape[0]
    half = HALF
    incl = iota((half, half), 1) <= iota((half, half), 0)
    c = jnp.broadcast_to(cols[:, n : n + 1], (tokens, half))
    c_row = cumul[n : n + 1, :]
    c_mid = c_row[:, half - 1 : half]
    d00 = jnp.where(incl, jnp.exp(c[:half] - c_row[:, :half]), 0.0)
    d11 = jnp.where(incl, jnp.exp(c[half:] - c_row[:, half:]), 0.0)
    d10 = jnp.exp(c[half:] - c_mid) * jnp.exp(c_mid - c_row[:, :half])
    return c, c_row, d00, d10, d11


def group_pairs(s, normed, weight, cumul, cols, pairs_ref, unit_keys, solved_ref):
    tokens, width = normed.shape
    heads_all = cumul.shape[0]
    half = HALF
    core, _ = place()
    ri = iota((half, half), 0)
    ci = iota((half, half), 1)
    strict = ci < ri
    eye = ri == ci
    pk = mm(normed[...], weight)
    heads = []
    for h in range(GROUP):
        n = s * GROUP + h
        if h % 2 == 0:
            at = h // 2 * 128
            raw = pk[:, at : at + 128]
            k = (raw * lax.rsqrt(jnp.sum(raw * raw, axis=-1, keepdims=True) + EPS)).astype(BF16)
            unit_keys[:, at : at + 128] = k
            kt = k.T
            g0 = mm(k[:half], kt[:, :half])
            g1 = mm(k[half:], kt)
            kf = k.astype(F32)
            ktf = kt.astype(F32)
        c, c_row, d00, d10, d11 = decays(n, cumul, cols)
        b = jnp.broadcast_to(cols[:, heads_all + n : heads_all + n + 1], (tokens, half))
        c_end = c_row[:, tokens - 1 : tokens]
        l00 = jnp.where(strict, b[:half] * d00 * g0, 0.0)
        l11 = jnp.where(strict, b[half:] * d11 * g1[:, half:], 0.0)
        l10 = (b[half:] * d10 * g1[:, :half]).astype(BF16)
        v_at = pl.multiple_of((n * 128 + (1 - core) * (width // 2)) % width, 128)
        v = normed[:, pl.ds(v_at, 128)].astype(F32)
        right = jnp.concatenate([(b * v).astype(BF16), (b * jnp.exp(c) * kf).astype(BF16)], axis=1)
        carried_t = (ktf * jnp.exp(c_end - c_row)).astype(BF16)
        heads.append((l00, l11, l10, right, carried_t, jnp.exp(c_end)))

    inverses = base_inverses([c for hd in heads for c in hd[:2]])
    couplings = [c for hd in heads for c in hd[:2]]
    m = BASE
    while m < half:
        inverses = merge(inverses, couplings, m)
        m *= 2

    tops = [mm(x, hd[3][:half]).astype(BF16) for x, hd in zip(inverses[::2], heads)]
    rests = [
        (hd[3][half:].astype(F32) - mm(hd[2], top)).astype(BF16) for hd, top in zip(heads, tops)
    ]
    lows = [mm(x, rest).astype(BF16) for x, rest in zip(inverses[1::2], rests)]
    for h in range(GROUP):
        solved = jnp.concatenate([tops[h], lows[h]], axis=0)
        solved_ref[h] = solved
        pair = mm(heads[h][4], solved)
        pairs_ref[h, 0] = (jnp.where(eye, heads[h][5], 0.0) - pair[:, 128:]).astype(BF16)
        pairs_ref[h, 1] = pair[:, :128].astype(BF16)


def first_kernel(
    x_hbm, gain_hbm, decay_hbm, rate_hbm, w_hbm,
    pairs_ref, unit_keys, solved_ref, xbuf, normed, wk, wq, cumul_ref, cols_ref,
    gains, logs_buf, rates_buf, sems,
):
    tokens, width = xbuf.shape
    steps = wk.shape[0]
    wcols = wk.shape[2]
    heads_all = logs_buf.shape[0]
    mid_head = heads_all // 2
    core, _ = place()
    here = pl.multiple_of(core * mid_head, mid_head)
    there = pl.multiple_of((1 - core) * mid_head, mid_head)
    pairs = [(gain_hbm, gains)]
    for at, frm in ((0, there), (mid_head, here)):
        pairs.append((decay_hbm.at[pl.ds(frm, mid_head)], logs_buf.at[pl.ds(at, mid_head)]))
        pairs.append((rate_hbm.at[pl.ds(frm, mid_head)], rates_buf.at[pl.ds(at, mid_head)]))
    x_at = len(pairs)
    rows = tokens // SPLIT
    for r in range(0, tokens, rows):
        pairs.append((x_hbm.at[pl.ds(r, rows)], xbuf.at[pl.ds(r, rows)]))
    w_at = len(pairs)
    rows = width // SPLIT
    for base, to in ((width // 2, wk), (0, wq)):
        for s in range(steps):
            frm = (s * wcols + (1 - core) * (width // 4)) % (width // 2)
            frm = pl.multiple_of(base + frm, 128)
            for r in range(0, width, rows):
                part = w_hbm.at[pl.ds(r, rows), pl.ds(frm, wcols)]
                pairs.append((part, to.at[s, pl.ds(r, rows)]))
    copies = fetch(pairs, sems)

    for copy in copies[:x_at]:
        copy.wait()
    upto = (iota((tokens, tokens), 0) <= iota((tokens, tokens), 1)).astype(BF16)
    hi, mid, low = split3(logs_buf[...])
    cumul = mm(hi, upto) + (mm(mid, upto) + mm(low, upto))
    cols = jnp.concatenate([cumul, rates_buf[...]], axis=0).T
    cumul_ref[...] = cumul
    cols_ref[...] = cols

    rows = tokens // SPLIT
    for n, r in enumerate(range(0, tokens, rows)):
        copies[x_at + n].wait()
        xf = xbuf[r : r + rows, :].astype(F32)
        normed[r : r + rows, :] = (
            xf * lax.rsqrt(jnp.mean(xf * xf, axis=-1, keepdims=True) + EPS) * gains[...]
        ).astype(BF16)

    for copy in copies[w_at : w_at + SPLIT]:
        copy.wait()
    group_pairs(0, normed, wk[0], cumul, cols, pairs_ref, unit_keys, solved_ref)
    for copy in copies[w_at + SPLIT :]:
        copy.wait()


def last_kernel(normed, wk, cumul_ref, cols_ref, pairs_ref, unit_keys, solved_ref):
    group_pairs(
        1, normed, wk[1], cumul_ref[...], cols_ref[...], pairs_ref, unit_keys, solved_ref
    )


def group_shapes(x, heads):
    tokens, width = x.shape
    return [
        jax.ShapeDtypeStruct((GROUP, 2, 128, 128), BF16),
        jax.ShapeDtypeStruct((tokens, GROUP // 2 * 128), BF16),
        jax.ShapeDtypeStruct((GROUP, tokens, 256), BF16),
    ]


def pairs_call(kernel, in_specs, outs, scratch, name, args):
    return pl.pallas_call(
        kernel,
        in_specs=in_specs,
        out_specs=[VMEM] * len(outs),
        out_shape=outs,
        scratch_shapes=scratch,
        compiler_params=pltpu.CompilerParams(vmem_limit_bytes=24 * 1024 * 1024),
        cost_estimate=pl.CostEstimate(
            flops=5_000_000_000, bytes_accessed=8_000_000, transcendentals=1_000_000
        ),
        name=name,
    )(*args)


def first_pairs(x, weight, gain_in, log_decay, write_rate):
    tokens, width = x.shape
    heads = log_decay.shape[0]
    steps = heads // GROUP
    wcols = GROUP // 2 * 128
    weights = jax.ShapeDtypeStruct((steps, width, wcols), BF16)
    return pairs_call(
        first_kernel,
        [pl.BlockSpec(memory_space=pltpu.HBM)] * 5,
        group_shapes(x, heads)
        + [
            jax.ShapeDtypeStruct((tokens, width), BF16),
            jax.ShapeDtypeStruct((tokens, width), BF16),
            weights,
            weights,
            jax.ShapeDtypeStruct((heads, tokens), F32),
            jax.ShapeDtypeStruct((tokens, 2 * heads), F32),
        ],
        [
            pltpu.VMEM((1, width), F32),
            pltpu.VMEM((heads, tokens), F32),
            pltpu.VMEM((heads, tokens), F32),
            pltpu.SemaphoreType.DMA((5 + (1 + 2 * steps) * SPLIT,)),
        ],
        "first_pairs",
        [in_hbm(a) for a in (x, gain_in, log_decay, write_rate, weight)],
    )


def last_pairs(normed, wk, cumul, cols):
    return pairs_call(
        last_kernel,
        [VMEM] * 4,
        group_shapes(normed, cumul.shape[0]),
        [],
        "last_pairs",
        (normed, wk, cumul, cols),
    )


def rows_kernel(s, normed, wq, unit_keys, solved_ref, cumul_ref, cols_ref, rows_ref):
    half = HALF
    tokens = normed.shape[0]
    pq = mm(normed[...], wq[s])
    cumul = cumul_ref[...]
    cols = cols_ref[...]
    heads = []
    for h in range(GROUP):
        n = s * GROUP + h
        if h % 2 == 0:
            at = h // 2 * 128
            q = pq[:, at : at + 128].astype(BF16)
            kt = unit_keys[:, at : at + 128].T
            g0 = mm(q[:half], kt[:, :half])
            g1 = mm(q[half:], kt)
            qf = q.astype(F32)
        c, _, d00, d10, d11 = decays(n, cumul, cols)
        s00 = (d00 * g0).astype(BF16)
        s1 = jnp.concatenate(
            [(d10 * g1[:, :half]).astype(BF16), (d11 * g1[:, half:]).astype(BF16)], axis=1
        )
        heads.append((s00, s1, jnp.exp(c) * qf))
    for h, (s00, s1, eq) in enumerate(heads):
        solved = solved_ref[h]
        out0 = mm(s00, solved[:half])
        out1 = mm(s1, solved)
        at = h * 128
        rows_ref[0, :half, at : at + 128] = (eq[:half] - out0[:, 128:]).astype(BF16)
        rows_ref[0, half:, at : at + 128] = (eq[half:] - out1[:, 128:]).astype(BF16)
        rows_ref[1, :half, at : at + 128] = out0[:, :128].astype(BF16)
        rows_ref[1, half:, at : at + 128] = out1[:, :128].astype(BF16)


def local_rows(s, *args):
    tokens = args[0].shape[0]
    return small_call(
        functools.partial(rows_kernel, s), [(2, tokens, GROUP * 128)], args, "local_rows"
    )[0]


def small_call(kernel, outs, args, name, scratch=()):
    return pl.pallas_call(
        kernel,
        in_specs=[VMEM] * len(args),
        out_specs=[VMEM] * len(outs),
        out_shape=[jax.ShapeDtypeStruct(shape, BF16) for shape in outs],
        scratch_shapes=list(scratch),
        compiler_params=pltpu.CompilerParams(vmem_limit_bytes=16 * 1024 * 1024),
        name=name,
    )(*args)


def compose_kernel(keep, other, *outs):
    core, chip = place()
    first = core == 0
    slots, early, late = [], [], []
    for shift, out in enumerate(outs):
        for i in range(out.shape[0]):
            h = (chip + shift) % XS * out.shape[0] + i
            mine, theirs = keep[h], other[h]
            slots.append((out, i))
            early.append(jnp.where(first, mine, theirs))
            late.append(jnp.where(first, theirs, mine))
    prods = [mm(b[0], jnp.concatenate([a[0], a[1]], axis=1)) for a, b in zip(early, late)]
    for (out, i), b, prod in zip(slots, late, prods):
        out[i, 0] = prod[:, :128].astype(BF16)
        out[i, 1] = (prod[:, 128:] + b[1].astype(F32)).astype(BF16)


def advance(pairs, states):
    his = [state.astype(BF16) for state in states]
    both = [
        jnp.concatenate([hi, (state - hi.astype(F32)).astype(BF16)], axis=1)
        for hi, state in zip(his, states)
    ]
    prods = [mm(pair[0], b) for pair, b in zip(pairs, both)]
    return [
        prod[:, :128] + prod[:, 128:] + pair[1].astype(F32) for pair, prod in zip(pairs, prods)
    ]


def total_kernel(*refs):
    parts, (ordered, total) = refs[:XS], refs[XS + 1 :]
    _, chip = place()
    for shift, part in enumerate(parts):
        ordered[(chip + XS - shift) % XS] = part[...]
    per = total.shape[0]
    states = [ordered[0, i, 1].astype(F32) for i in range(per)]
    for j in range(1, XS):
        states = advance([ordered[j, i] for i in range(per)], states)
    for i in range(per):
        total[i] = states[i].astype(BF16)


def split2(value):
    hi = value.astype(BF16)
    return hi, (value - hi.astype(F32)).astype(BF16)


def row_kernel(ordered, trans, state):
    shape = trans.shape
    per = shape[1]
    pairs = [
        jnp.concatenate([ordered[0, i, 0], ordered[0, i, 1]], axis=1).astype(F32)
        for i in range(per)
    ]
    for j in range(shape[0]):
        if j:
            both = [jnp.concatenate(split2(p), axis=1) for p in pairs]
            prods = [mm(ordered[j, i, 0], b) for i, b in enumerate(both)]
            sums = [p[:, :256] + p[:, 256:] for p in prods]
            pairs = [
                jnp.concatenate([p[:, :128], p[:, 128:] + ordered[j, i, 1].astype(F32)], axis=1)
                for i, p in enumerate(sums)
            ]
        for i, p in enumerate(pairs):
            hi, low = split2(p)
            trans[j, i, :128], trans[j, i, 128:] = hi[:, :128], low[:, :128]
            state[j, i, :128], state[j, i, 128:] = hi[:, 128:], low[:, 128:]


def starts_kernel(trans, state, before, _, *refs):
    outs, scratch = refs[:XS], refs[XS]
    _, chip = place()
    per = before.shape[0]
    places = [(j, i) for j in range(XS - 1) for i in range(per)]
    prods = [mm(trans[j, i], before[i]) for j, i in places]
    for i in range(per):
        scratch[(XS - chip) % XS, i] = before[i]
    for (j, i), prod in zip(places, prods):
        extra = state[j, i, :128].astype(F32) + state[j, i, 128:].astype(F32)
        value = prod[:128] + prod[128:] + extra
        scratch[(j + 1 + XS - chip) % XS, i] = value.astype(BF16)
    for shift, out in enumerate(outs):
        out[...] = scratch[shift]


def finish_heads(rows_ref, rows_at, states, x_ref, x_at, gain, out_ref):
    where = [pl.ds(pl.multiple_of(at, 128), 128) for at in rows_at]
    mixed = [mm(rows_ref[0, :, w], state) for w, state in zip(where, states)]
    mixed = [m + rows_ref[1, :, w].astype(F32) for m, w in zip(mixed, where)]
    scales = [lax.rsqrt(jnp.mean(m * m, axis=-1, keepdims=True) + EPS) for m in mixed]
    for n, (m, scale, at) in enumerate(zip(mixed, scales, x_at)):
        rows = x_ref[:, pl.ds(pl.multiple_of(at, 128), 128)].astype(F32)
        branch = (m * scale * gain).astype(BF16).astype(F32)
        out_ref[:, n * 128 : n * 128 + 128] = (rows + branch).astype(BF16)


def looked_after(parts, shifts, keep, other):
    core, chip = place()
    first = core == 0
    heads, starts = [], []
    for shift, part in zip(shifts, parts):
        for i in range(part.shape[0]):
            heads.append((chip + XS - shift) % XS * part.shape[0] + i)
            starts.append(part[i])
    early = [jnp.where(first, keep[h], other[h]) for h in heads]
    after = [mm(e[0], start) for e, start in zip(early, starts)]
    after = [(a + e[1].astype(F32)).astype(BF16) for a, e in zip(after, early)]
    mine = [jnp.where(first, a, b) for a, b in zip(starts, after)]
    theirs = [jnp.where(first, b, a) for a, b in zip(starts, after)]
    return heads, mine, theirs


def near_heads(parts, shifts, keep, other, near, x_ref, gain_ref, out_ref):
    core, _ = place()
    mid = x_ref.shape[1] // 2
    heads, mine, _ = looked_after(parts, shifts, keep, other)
    rows_at = [h * 128 for h in heads]
    x_at = [core * mid + h * 128 for h in heads]
    finish_heads(near, rows_at, mine, x_ref, x_at, gain_ref[...], out_ref)


def near_own_kernel(part, *refs):
    near_heads([part], [0], *refs)


def near_rest_kernel(*refs):
    near_heads(refs[: XS - 1], range(1, XS), *refs[XS - 1 :])


def theirs_kernel(*refs):
    parts, (keep, other, _, theirs) = refs[:XS], refs[XS:]
    heads, _, states = looked_after(parts, range(XS), keep, other)
    for h, state in zip(heads, states):
        theirs[h] = state


def far_kernel(first, far, got, x_ref, gain_ref, _, out_ref):
    core, _ = place()
    mid = x_ref.shape[1] // 2
    heads = range(first, first + out_ref.shape[1] // 128)
    rows_at = [h * 128 for h in heads]
    x_at = [(1 - core) * mid + at for at in rows_at]
    finish_heads(far, rows_at, [got[h] for h in heads], x_ref, x_at, gain_ref[...], out_ref)


def place_kernel(own, rest, far1, out_hbm, sems):
    core, chip = place()
    mid = out_hbm.shape[1] // 2
    per = own.shape[1]

    def columns(at, size):
        return out_hbm.at[:, pl.ds(pl.multiple_of(at, 128), size)]

    pairs = [(own, columns(core * mid + chip * per, per))]
    for shift in range(1, XS):
        part = rest.at[:, pl.ds((shift - 1) * per, per)]
        pairs.append((part, columns(core * mid + (chip + XS - shift) % XS * per, per)))
    pairs.append((far1, columns((1 - core) * mid, far1.shape[1])))
    for copy in fetch(pairs, sems):
        copy.wait()


def place_last_kernel(far2, _, out_hbm, sems):
    core, _ = place()
    cols = far2.shape[1]
    at = pl.multiple_of((1 - core) * 2 * cols + cols, 128)
    for copy in fetch([(far2, out_hbm.at[:, pl.ds(at, cols)])], sems):
        copy.wait()


def place_columns(width, kernel, parts, name, out=None):
    hbm = pl.BlockSpec(memory_space=pltpu.HBM)
    last = () if out is None else (out,)
    return pl.pallas_call(
        kernel,
        in_specs=[VMEM] * len(parts) + [hbm] * len(last),
        out_specs=hbm,
        out_shape=jax.ShapeDtypeStruct((parts[0].shape[0], width), BF16),
        scratch_shapes=[pltpu.SemaphoreType.DMA((XS + 1,))],
        input_output_aliases={len(parts): 0} if last else {},
        compiler_params=pltpu.CompilerParams(vmem_limit_bytes=16 * 1024 * 1024),
        name=name,
    )(*parts, *last)


def swap_cores(array):
    return lax.ppermute(array, "ctx", [(i, i ^ 1) for i in range(lax.axis_size("ctx"))])


def along_x(array, shift):
    pairs = []
    for i in range(lax.axis_size("ctx")):
        row, chip, core = i // (2 * XS), i // 2 % XS, i % 2
        pairs.append((i, (row * XS + (chip + shift) % XS) * 2 + core))
    return lax.ppermute(array, "ctx", pairs)


def row_starts(keep, other, near, far):
    per = keep.shape[0] // XS
    parts = small_call(compose_kernel, [(per, 2, 128, 128)] * XS, (keep, other), "compose")
    parts = [parts[0]] + [along_x(parts[r], r) for r in range(1, XS)]
    ordered, total = small_call(
        total_kernel, [(XS, per, 2, 128, 128), (per, 128, 128)], (*parts, near), "row_total"
    )
    row = 2 * XS
    before = lax.ppermute(total, "ctx", [(i, i + row) for i in range(row)])
    row_pairs = small_call(row_kernel, [(XS - 1, per, 256, 128)] * 2, (ordered,), "row_pairs")
    starts = small_call(
        starts_kernel,
        [(per, 128, 128)] * XS,
        (*row_pairs, before, far),
        "row_starts",
        [pltpu.VMEM((XS, per, 128, 128), BF16)],
    )
    return starts[0], [along_x(starts[r], r) for r in range(1, XS)]


def next_section(array):
    n = lax.axis_size("section")
    return lax.ppermute(array, "section", [(i, (i + 1) % n) for i in range(n)])


def on_device(layer_input, qk_weight, norm_gain, out_gain, log_decay, write_rate):
    send, far_keys, far_solved, x, normed, wk, wq, cumul, cols = first_pairs(
        layer_input[0], qk_weight[0], norm_gain, log_decay[0], write_rate[0]
    )
    other = swap_cores(send)
    keep, near_keys, near_solved = last_pairs(normed, wk, cumul, cols)
    near = local_rows(1, normed, wq, near_keys, near_solved, cumul, cols)
    far = local_rows(0, normed, wq, far_keys, far_solved, cumul, cols)
    own, rest = row_starts(keep, other, near, far)
    tokens, width = x.shape
    per = width // 2 // XS
    common = (keep, other, near, x, out_gain)
    done_own = small_call(near_own_kernel, [(tokens, per)], (own, *common), "finish_own")[0]
    done_own = next_section(done_own)
    done_rest = small_call(
        near_rest_kernel, [(tokens, (XS - 1) * per)], (*rest, *common), "finish_rest"
    )[0]
    done_rest = next_section(done_rest)
    theirs = small_call(
        theirs_kernel,
        [(keep.shape[0], 128, 128)],
        (own, *rest, keep, other, done_own),
        "other_core",
    )[0]
    got = swap_cores(theirs)

    def finish_far(first, after):
        done = small_call(
            functools.partial(far_kernel, first),
            [(tokens, width // 4)],
            (far, got, x, out_gain, after),
            "finish_far",
        )[0]
        return next_section(done)

    done_far1 = finish_far(0, done_own)
    done_far2 = finish_far(keep.shape[0] // 2, done_rest)
    most = place_columns(width, place_kernel, (done_own, done_rest, done_far1), "place_most")
    return place_columns(width, place_last_kernel, (done_far2,), "place_last", most)[None]


def solution(mesh):
    in_specs = (
        P("section", "ctx", None),
        P("section", None, None),
        P("section", None),
        P("section", None),
        P("section", None, "ctx"),
        P("section", None, "ctx"),
    )
    out_specs = P("section", "ctx", None)
    return jax.shard_map(
        on_device, mesh=mesh, in_specs=in_specs, out_specs=out_specs, check_vma=False
    )
```

```python
import functools

import jax
import jax.numpy as jnp
from jax import lax
from jax.experimental import pallas as pl
from jax.experimental.pallas import tpu as pltpu
from jax.sharding import PartitionSpec as P

F32 = jnp.float32
BF16 = jnp.bfloat16
EPS = 1e-6
HALF = 128
BASE = 8
GROUP = 8
XS = 4
FAR = 5
SPLIT = 4
VMEM = pl.BlockSpec(memory_space=pltpu.VMEM)


def in_hbm(array):
    return pltpu.with_memory_space_constraint(array, pltpu.HBM)


def place():
    at = lax.axis_index("ctx")
    return at % 2, at // 2 % XS


def mm(a, b):
    return jnp.dot(a, b, preferred_element_type=F32)


def iota(shape, dim):
    return lax.broadcasted_iota(jnp.int32, shape, dim)


def base_inverses(couplings):
    lanes = HALF
    count = len(couplings)
    blocks = lanes // BASE
    lane = iota((BASE, lanes), 1)
    packed = []
    for c in couplings:
        d = jnp.zeros((BASE, lanes), F32)
        for blk in range(blocks):
            d = jnp.where(lane // BASE == blk, c[blk * BASE : (blk + 1) * BASE, :], d)
        packed.append(d)
    d = jnp.concatenate(packed, axis=0)
    rows = count * BASE
    lane_all = iota((rows, lanes), 1)
    x = jnp.where(iota((rows, lanes), 0) % BASE == lane_all % BASE, 1.0, 0.0).astype(F32)
    x = x.reshape(count, BASE, lanes)
    for j in range(BASE - 1):
        spread = jnp.take_along_axis(d, lane_all // BASE * BASE + j, axis=1)
        x = x - spread.reshape(count, BASE, lanes) * x[:, j : j + 1, :]
    full = []
    for n in range(count):
        full.append(
            jnp.concatenate(
                [jnp.where(lane // BASE == blk, x[n], 0.0) for blk in range(blocks)], axis=0
            )
        )
    return full


def merge(inverses, couplings, m):
    kind = F32 if m < 16 else BF16
    size = HALF
    pairs = size // (2 * m)
    lane = iota((m, size), 1)
    odd_at = [(2 * p + 1) * m for p in range(pairs)]
    couplings = [c.astype(kind) for c in couplings]
    left = [
        jnp.concatenate(
            [
                jnp.where(lane // m == 2 * p, c[at : at + m, :], jnp.zeros((), kind))
                for p, at in enumerate(odd_at)
            ],
            axis=0,
        ).astype(BF16)
        for c in couplings
    ]
    middle = [mm(a, x.astype(BF16)).astype(kind) for a, x in zip(left, inverses)]
    blank = jnp.zeros((m, size), kind)
    spread = [
        jnp.concatenate(
            [part for p in range(pairs) for part in (blank, y[p * m : (p + 1) * m, :])], axis=0
        ).astype(BF16)
        for y in middle
    ]
    odd = [jnp.concatenate([x[at : at + m, :] for at in odd_at], axis=0) for x in inverses]
    lower = [mm(a.astype(BF16), y).astype(kind) for a, y in zip(odd, spread)]
    return [
        jnp.concatenate(
            [
                part
                for p, at in enumerate(odd_at)
                for part in (x[at - m : at, :], (o - z)[p * m : (p + 1) * m, :])
            ],
            axis=0,
        ).astype(BF16)
        for x, o, z in zip(inverses, odd, lower)
    ]


def split3(value):
    hi = value.astype(BF16)
    rest = value - hi.astype(F32)
    mid = rest.astype(BF16)
    return hi, mid, (rest - mid.astype(F32)).astype(BF16)


def fetch(pairs, sems):
    copies = [pltpu.make_async_copy(a, b, sems.at[n]) for n, (a, b) in enumerate(pairs)]
    for copy in copies:
        copy.start()
    return copies


def decays(n, cumul, cols):
    tokens = cols.shape[0]
    half = HALF
    incl = iota((half, half), 1) <= iota((half, half), 0)
    c = jnp.broadcast_to(cols[:, n : n + 1], (tokens, half))
    c_row = cumul[n : n + 1, :]
    c_mid = c_row[:, half - 1 : half]
    d00 = jnp.where(incl, jnp.exp(c[:half] - c_row[:, :half]), 0.0)
    d11 = jnp.where(incl, jnp.exp(c[half:] - c_row[:, half:]), 0.0)
    d10 = jnp.exp(c[half:] - c_mid) * jnp.exp(c_mid - c_row[:, :half])
    return c, c_row, d00, d10, d11


def group_pairs(s, normed, weight, cumul, cols, pairs_ref, unit_keys, solved_ref):
    tokens, width = normed.shape
    heads_all = cumul.shape[0]
    half = HALF
    core, _ = place()
    ri = iota((half, half), 0)
    ci = iota((half, half), 1)
    strict = ci < ri
    eye = ri == ci
    pk = mm(normed[...], weight)
    heads = []
    for h in range(GROUP):
        n = s * GROUP + h
        if h % 2 == 0:
            at = h // 2 * 128
            raw = pk[:, at : at + 128]
            k = (raw * lax.rsqrt(jnp.sum(raw * raw, axis=-1, keepdims=True) + EPS)).astype(BF16)
            unit_keys[:, at : at + 128] = k
            kt = k.T
            g0 = mm(k[:half], kt[:, :half])
            g1 = mm(k[half:], kt)
            kf = k.astype(F32)
            ktf = kt.astype(F32)
        c, c_row, d00, d10, d11 = decays(n, cumul, cols)
        b = jnp.broadcast_to(cols[:, heads_all + n : heads_all + n + 1], (tokens, half))
        c_end = c_row[:, tokens - 1 : tokens]
        l00 = jnp.where(strict, b[:half] * d00 * g0, 0.0)
        l11 = jnp.where(strict, b[half:] * d11 * g1[:, half:], 0.0)
        l10 = (b[half:] * d10 * g1[:, :half]).astype(BF16)
        v_at = pl.multiple_of((n * 128 + (1 - core) * (width // 2)) % width, 128)
        v = normed[:, pl.ds(v_at, 128)].astype(F32)
        right = jnp.concatenate([(b * v).astype(BF16), (b * jnp.exp(c) * kf).astype(BF16)], axis=1)
        carried_t = (ktf * jnp.exp(c_end - c_row)).astype(BF16)
        heads.append((l00, l11, l10, right, carried_t, jnp.exp(c_end)))

    inverses = base_inverses([c for hd in heads for c in hd[:2]])
    couplings = [c for hd in heads for c in hd[:2]]
    m = BASE
    while m < half:
        inverses = merge(inverses, couplings, m)
        m *= 2

    tops = [mm(x, hd[3][:half]).astype(BF16) for x, hd in zip(inverses[::2], heads)]
    rests = [
        (hd[3][half:].astype(F32) - mm(hd[2], top)).astype(BF16) for hd, top in zip(heads, tops)
    ]
    lows = [mm(x, rest).astype(BF16) for x, rest in zip(inverses[1::2], rests)]
    for h in range(GROUP):
        solved = jnp.concatenate([tops[h], lows[h]], axis=0)
        solved_ref[h] = solved
        pair = mm(heads[h][4], solved)
        pairs_ref[h, 0] = (jnp.where(eye, heads[h][5], 0.0) - pair[:, 128:]).astype(BF16)
        pairs_ref[h, 1] = pair[:, :128].astype(BF16)


def first_kernel(
    x_hbm, gain_hbm, decay_hbm, rate_hbm, w_hbm,
    pairs_ref, unit_keys, solved_ref, xbuf, normed, wk, wq, cumul_ref, cols_ref,
    gains, logs_buf, rates_buf, sems,
):
    tokens, width = xbuf.shape
    steps = wk.shape[0]
    wcols = wk.shape[2]
    heads_all = logs_buf.shape[0]
    mid_head = heads_all // 2
    core, _ = place()
    here = pl.multiple_of(core * mid_head, mid_head)
    there = pl.multiple_of((1 - core) * mid_head, mid_head)
    pairs = [(gain_hbm, gains)]
    for at, frm in ((0, there), (mid_head, here)):
        pairs.append((decay_hbm.at[pl.ds(frm, mid_head)], logs_buf.at[pl.ds(at, mid_head)]))
        pairs.append((rate_hbm.at[pl.ds(frm, mid_head)], rates_buf.at[pl.ds(at, mid_head)]))
    x_at = len(pairs)
    rows = tokens // SPLIT
    for r in range(0, tokens, rows):
        pairs.append((x_hbm.at[pl.ds(r, rows)], xbuf.at[pl.ds(r, rows)]))
    w_at = len(pairs)
    rows = width // SPLIT
    for base, to in ((width // 2, wk), (0, wq)):
        for s in range(steps):
            frm = (s * wcols + (1 - core) * (width // 4)) % (width // 2)
            frm = pl.multiple_of(base + frm, 128)
            for r in range(0, width, rows):
                part = w_hbm.at[pl.ds(r, rows), pl.ds(frm, wcols)]
                pairs.append((part, to.at[s, pl.ds(r, rows)]))
    copies = fetch(pairs, sems)

    for copy in copies[:x_at]:
        copy.wait()
    upto = (iota((tokens, tokens), 0) <= iota((tokens, tokens), 1)).astype(BF16)
    hi, mid, low = split3(logs_buf[...])
    cumul = mm(hi, upto) + (mm(mid, upto) + mm(low, upto))
    cols = jnp.concatenate([cumul, rates_buf[...]], axis=0).T
    cumul_ref[...] = cumul
    cols_ref[...] = cols

    rows = tokens // SPLIT
    for n, r in enumerate(range(0, tokens, rows)):
        copies[x_at + n].wait()
        xf = xbuf[r : r + rows, :].astype(F32)
        normed[r : r + rows, :] = (
            xf * lax.rsqrt(jnp.mean(xf * xf, axis=-1, keepdims=True) + EPS) * gains[...]
        ).astype(BF16)

    for copy in copies[w_at : w_at + SPLIT]:
        copy.wait()
    group_pairs(0, normed, wk[0], cumul, cols, pairs_ref, unit_keys, solved_ref)
    for copy in copies[w_at + SPLIT :]:
        copy.wait()


def last_kernel(normed, wk, cumul_ref, cols_ref, pairs_ref, unit_keys, solved_ref):
    group_pairs(
        1, normed, wk[1], cumul_ref[...], cols_ref[...], pairs_ref, unit_keys, solved_ref
    )


def group_shapes(x, heads):
    tokens, width = x.shape
    return [
        jax.ShapeDtypeStruct((GROUP, 2, 128, 128), BF16),
        jax.ShapeDtypeStruct((tokens, GROUP // 2 * 128), BF16),
        jax.ShapeDtypeStruct((GROUP, tokens, 256), BF16),
    ]


def pairs_call(kernel, in_specs, outs, scratch, name, args):
    return pl.pallas_call(
        kernel,
        in_specs=in_specs,
        out_specs=[VMEM] * len(outs),
        out_shape=outs,
        scratch_shapes=scratch,
        compiler_params=pltpu.CompilerParams(vmem_limit_bytes=24 * 1024 * 1024),
        cost_estimate=pl.CostEstimate(
            flops=5_000_000_000, bytes_accessed=8_000_000, transcendentals=1_000_000
        ),
        name=name,
    )(*args)


def first_pairs(x, weight, gain_in, log_decay, write_rate):
    tokens, width = x.shape
    heads = log_decay.shape[0]
    steps = heads // GROUP
    wcols = GROUP // 2 * 128
    weights = jax.ShapeDtypeStruct((steps, width, wcols), BF16)
    return pairs_call(
        first_kernel,
        [pl.BlockSpec(memory_space=pltpu.HBM)] * 5,
        group_shapes(x, heads)
        + [
            jax.ShapeDtypeStruct((tokens, width), BF16),
            jax.ShapeDtypeStruct((tokens, width), BF16),
            weights,
            weights,
            jax.ShapeDtypeStruct((heads, tokens), F32),
            jax.ShapeDtypeStruct((tokens, 2 * heads), F32),
        ],
        [
            pltpu.VMEM((1, width), F32),
            pltpu.VMEM((heads, tokens), F32),
            pltpu.VMEM((heads, tokens), F32),
            pltpu.SemaphoreType.DMA((5 + (1 + 2 * steps) * SPLIT,)),
        ],
        "first_pairs",
        [in_hbm(a) for a in (x, gain_in, log_decay, write_rate, weight)],
    )


def last_pairs(normed, wk, cumul, cols):
    return pairs_call(
        last_kernel,
        [VMEM] * 4,
        group_shapes(normed, cumul.shape[0]),
        [],
        "last_pairs",
        (normed, wk, cumul, cols),
    )


def rows_kernel(s, normed, wq, unit_keys, solved_ref, cumul_ref, cols_ref, rows_ref):
    half = HALF
    tokens = normed.shape[0]
    pq = mm(normed[...], wq[s])
    cumul = cumul_ref[...]
    cols = cols_ref[...]
    heads = []
    for h in range(GROUP):
        n = s * GROUP + h
        if h % 2 == 0:
            at = h // 2 * 128
            q = pq[:, at : at + 128].astype(BF16)
            kt = unit_keys[:, at : at + 128].T
            g0 = mm(q[:half], kt[:, :half])
            g1 = mm(q[half:], kt)
            qf = q.astype(F32)
        c, _, d00, d10, d11 = decays(n, cumul, cols)
        s00 = (d00 * g0).astype(BF16)
        s1 = jnp.concatenate(
            [(d10 * g1[:, :half]).astype(BF16), (d11 * g1[:, half:]).astype(BF16)], axis=1
        )
        heads.append((s00, s1, jnp.exp(c) * qf))
    for h, (s00, s1, eq) in enumerate(heads):
        solved = solved_ref[h]
        out0 = mm(s00, solved[:half])
        out1 = mm(s1, solved)
        at = h * 128
        rows_ref[0, :half, at : at + 128] = (eq[:half] - out0[:, 128:]).astype(BF16)
        rows_ref[0, half:, at : at + 128] = (eq[half:] - out1[:, 128:]).astype(BF16)
        rows_ref[1, :half, at : at + 128] = out0[:, :128].astype(BF16)
        rows_ref[1, half:, at : at + 128] = out1[:, :128].astype(BF16)


def local_rows(s, *args):
    tokens = args[0].shape[0]
    return small_call(
        functools.partial(rows_kernel, s), [(2, tokens, GROUP * 128)], args, "local_rows"
    )[0]


def small_call(kernel, outs, args, name, scratch=()):
    return pl.pallas_call(
        kernel,
        in_specs=[VMEM] * len(args),
        out_specs=[VMEM] * len(outs),
        out_shape=[jax.ShapeDtypeStruct(shape, BF16) for shape in outs],
        scratch_shapes=list(scratch),
        compiler_params=pltpu.CompilerParams(vmem_limit_bytes=16 * 1024 * 1024),
        name=name,
    )(*args)


def compose_kernel(keep, other, *outs):
    core, chip = place()
    first = core == 0
    slots, early, late = [], [], []
    for shift, out in enumerate(outs):
        for i in range(out.shape[0]):
            h = (chip + shift) % XS * out.shape[0] + i
            mine, theirs = keep[h], other[h]
            slots.append((out, i))
            early.append(jnp.where(first, mine, theirs))
            late.append(jnp.where(first, theirs, mine))
    prods = [mm(b[0], jnp.concatenate([a[0], a[1]], axis=1)) for a, b in zip(early, late)]
    for (out, i), b, prod in zip(slots, late, prods):
        out[i, 0] = prod[:, :128].astype(BF16)
        out[i, 1] = (prod[:, 128:] + b[1].astype(F32)).astype(BF16)


def advance(pairs, states):
    his = [state.astype(BF16) for state in states]
    both = [
        jnp.concatenate([hi, (state - hi.astype(F32)).astype(BF16)], axis=1)
        for hi, state in zip(his, states)
    ]
    prods = [mm(pair[0], b) for pair, b in zip(pairs, both)]
    return [
        prod[:, :128] + prod[:, 128:] + pair[1].astype(F32) for pair, prod in zip(pairs, prods)
    ]


def total_kernel(*refs):
    parts, (ordered, total) = refs[:XS], refs[XS + 1 :]
    _, chip = place()
    for shift, part in enumerate(parts):
        ordered[(chip + XS - shift) % XS] = part[...]
    per = total.shape[0]
    states = [ordered[0, i, 1].astype(F32) for i in range(per)]
    for j in range(1, XS):
        states = advance([ordered[j, i] for i in range(per)], states)
    for i in range(per):
        total[i] = states[i].astype(BF16)


def split2(value):
    hi = value.astype(BF16)
    return hi, (value - hi.astype(F32)).astype(BF16)


def row_kernel(ordered, trans, state):
    shape = trans.shape
    per = shape[1]
    pairs = [
        jnp.concatenate([ordered[0, i, 0], ordered[0, i, 1]], axis=1).astype(F32)
        for i in range(per)
    ]
    for j in range(shape[0]):
        if j:
            both = [jnp.concatenate(split2(p), axis=1) for p in pairs]
            prods = [mm(ordered[j, i, 0], b) for i, b in enumerate(both)]
            sums = [p[:, :256] + p[:, 256:] for p in prods]
            pairs = [
                jnp.concatenate([p[:, :128], p[:, 128:] + ordered[j, i, 1].astype(F32)], axis=1)
                for i, p in enumerate(sums)
            ]
        for i, p in enumerate(pairs):
            hi, low = split2(p)
            trans[j, i, :128], trans[j, i, 128:] = hi[:, :128], low[:, :128]
            state[j, i, :128], state[j, i, 128:] = hi[:, 128:], low[:, 128:]


def starts_kernel(trans, state, before, _, *refs):
    outs, scratch = refs[:XS], refs[XS]
    _, chip = place()
    per = before.shape[0]
    places = [(j, i) for j in range(XS - 1) for i in range(per)]
    prods = [mm(trans[j, i], before[i]) for j, i in places]
    for i in range(per):
        scratch[(XS - chip) % XS, i] = before[i]
    for (j, i), prod in zip(places, prods):
        extra = state[j, i, :128].astype(F32) + state[j, i, 128:].astype(F32)
        value = prod[:128] + prod[128:] + extra
        scratch[(j + 1 + XS - chip) % XS, i] = value.astype(BF16)
    for shift, out in enumerate(outs):
        out[...] = scratch[shift]


def finish_heads(rows_ref, rows_at, states, x_ref, x_at, gain, out_ref):
    where = [pl.ds(pl.multiple_of(at, 128), 128) for at in rows_at]
    mixed = [mm(rows_ref[0, :, w], state) for w, state in zip(where, states)]
    mixed = [m + rows_ref[1, :, w].astype(F32) for m, w in zip(mixed, where)]
    scales = [lax.rsqrt(jnp.mean(m * m, axis=-1, keepdims=True) + EPS) for m in mixed]
    for n, (m, scale, at) in enumerate(zip(mixed, scales, x_at)):
        rows = x_ref[:, pl.ds(pl.multiple_of(at, 128), 128)].astype(F32)
        branch = (m * scale * gain).astype(BF16).astype(F32)
        out_ref[:, n * 128 : n * 128 + 128] = (rows + branch).astype(BF16)


def looked_after(parts, shifts, keep, other):
    core, chip = place()
    first = core == 0
    heads, starts = [], []
    for shift, part in zip(shifts, parts):
        for i in range(part.shape[0]):
            heads.append((chip + XS - shift) % XS * part.shape[0] + i)
            starts.append(part[i])
    early = [jnp.where(first, keep[h], other[h]) for h in heads]
    after = [mm(e[0], start) for e, start in zip(early, starts)]
    after = [(a + e[1].astype(F32)).astype(BF16) for a, e in zip(after, early)]
    mine = [jnp.where(first, a, b) for a, b in zip(starts, after)]
    theirs = [jnp.where(first, b, a) for a, b in zip(starts, after)]
    return heads, mine, theirs


def near_heads(parts, shifts, keep, other, near, x_ref, gain_ref, out_ref):
    core, _ = place()
    mid = x_ref.shape[1] // 2
    heads, mine, _ = looked_after(parts, shifts, keep, other)
    rows_at = [h * 128 for h in heads]
    x_at = [core * mid + h * 128 for h in heads]
    finish_heads(near, rows_at, mine, x_ref, x_at, gain_ref[...], out_ref)


def near_own_kernel(part, *refs):
    near_heads([part], [0], *refs)


def near_rest_kernel(*refs):
    near_heads(refs[: XS - 1], range(1, XS), *refs[XS - 1 :])


def theirs_kernel(*refs):
    parts, (keep, other, _, theirs) = refs[:XS], refs[XS:]
    heads, _, states = looked_after(parts, range(XS), keep, other)
    for h, state in zip(heads, states):
        theirs[h] = state


def far_kernel(first, far, got, x_ref, gain_ref, _, out_ref):
    core, _ = place()
    mid = x_ref.shape[1] // 2
    heads = range(first, first + out_ref.shape[1] // 128)
    rows_at = [h * 128 for h in heads]
    x_at = [(1 - core) * mid + at for at in rows_at]
    finish_heads(far, rows_at, [got[h] for h in heads], x_ref, x_at, gain_ref[...], out_ref)


def place_kernel(own, rest, far1, out_hbm, sems):
    core, chip = place()
    mid = out_hbm.shape[1] // 2
    per = own.shape[1]

    def columns(at, size):
        return out_hbm.at[:, pl.ds(pl.multiple_of(at, 128), size)]

    pairs = [(own, columns(core * mid + chip * per, per))]
    for shift in range(1, XS):
        part = rest.at[:, pl.ds((shift - 1) * per, per)]
        pairs.append((part, columns(core * mid + (chip + XS - shift) % XS * per, per)))
    pairs.append((far1, columns((1 - core) * mid, far1.shape[1])))
    for copy in fetch(pairs, sems):
        copy.wait()


def place_last_kernel(far2, _, out_hbm, sems):
    core, _ = place()
    cols = far2.shape[1]
    mid = out_hbm.shape[1] // 2
    at = pl.multiple_of((1 - core) * mid + mid - cols, 128)
    for copy in fetch([(far2, out_hbm.at[:, pl.ds(at, cols)])], sems):
        copy.wait()


def place_columns(width, kernel, parts, name, out=None):
    hbm = pl.BlockSpec(memory_space=pltpu.HBM)
    last = () if out is None else (out,)
    return pl.pallas_call(
        kernel,
        in_specs=[VMEM] * len(parts) + [hbm] * len(last),
        out_specs=hbm,
        out_shape=jax.ShapeDtypeStruct((parts[0].shape[0], width), BF16),
        scratch_shapes=[pltpu.SemaphoreType.DMA((XS + 1,))],
        input_output_aliases={len(parts): 0} if last else {},
        compiler_params=pltpu.CompilerParams(vmem_limit_bytes=16 * 1024 * 1024),
        name=name,
    )(*parts, *last)


def swap_cores(array):
    return lax.ppermute(array, "ctx", [(i, i ^ 1) for i in range(lax.axis_size("ctx"))])


def along_x(array, shift):
    pairs = []
    for i in range(lax.axis_size("ctx")):
        row, chip, core = i // (2 * XS), i // 2 % XS, i % 2
        pairs.append((i, (row * XS + (chip + shift) % XS) * 2 + core))
    return lax.ppermute(array, "ctx", pairs)


def row_starts(keep, other, near, far):
    per = keep.shape[0] // XS
    parts = small_call(compose_kernel, [(per, 2, 128, 128)] * XS, (keep, other), "compose")
    parts = [parts[0]] + [along_x(parts[r], r) for r in range(1, XS)]
    ordered, total = small_call(
        total_kernel, [(XS, per, 2, 128, 128), (per, 128, 128)], (*parts, near), "row_total"
    )
    row = 2 * XS
    before = lax.ppermute(total, "ctx", [(i, i + row) for i in range(row)])
    row_pairs = small_call(row_kernel, [(XS - 1, per, 256, 128)] * 2, (ordered,), "row_pairs")
    starts = small_call(
        starts_kernel,
        [(per, 128, 128)] * XS,
        (*row_pairs, before, far),
        "row_starts",
        [pltpu.VMEM((XS, per, 128, 128), BF16)],
    )
    return starts[0], [along_x(starts[r], r) for r in range(1, XS)]


def next_section(array):
    n = lax.axis_size("section")
    return lax.ppermute(array, "section", [(i, (i + 1) % n) for i in range(n)])


def on_device(layer_input, qk_weight, norm_gain, out_gain, log_decay, write_rate):
    send, far_keys, far_solved, x, normed, wk, wq, cumul, cols = first_pairs(
        layer_input[0], qk_weight[0], norm_gain, log_decay[0], write_rate[0]
    )
    other = swap_cores(send)
    keep, near_keys, near_solved = last_pairs(normed, wk, cumul, cols)
    near = local_rows(1, normed, wq, near_keys, near_solved, cumul, cols)
    far = local_rows(0, normed, wq, far_keys, far_solved, cumul, cols)
    own, rest = row_starts(keep, other, near, far)
    tokens, width = x.shape
    per = width // 2 // XS
    common = (keep, other, near, x, out_gain)
    done_own = small_call(near_own_kernel, [(tokens, per)], (own, *common), "finish_own")[0]
    done_own = next_section(done_own)
    done_rest = small_call(
        near_rest_kernel, [(tokens, (XS - 1) * per)], (*rest, *common), "finish_rest"
    )[0]
    done_rest = next_section(done_rest)
    theirs = small_call(
        theirs_kernel,
        [(keep.shape[0], 128, 128)],
        (own, *rest, keep, other, done_own),
        "other_core",
    )[0]
    got = swap_cores(theirs)

    def finish_far(first, count, after):
        done = small_call(
            functools.partial(far_kernel, first),
            [(tokens, count * 128)],
            (far, got, x, out_gain, after),
            "finish_far",
        )[0]
        return next_section(done)

    done_far1 = finish_far(0, FAR, done_own)
    done_far2 = finish_far(FAR, keep.shape[0] - FAR, done_rest)
    most = place_columns(width, place_kernel, (done_own, done_rest, done_far1), "place_most")
    return place_columns(width, place_last_kernel, (done_far2,), "place_last", most)[None]


def solution(mesh):
    in_specs = (
        P("section", "ctx", None),
        P("section", None, None),
        P("section", None),
        P("section", None),
        P("section", None, "ctx"),
        P("section", None, "ctx"),
    )
    out_specs = P("section", "ctx", None)
    return jax.shard_map(
        on_device, mesh=mesh, in_specs=in_specs, out_specs=out_specs, check_vma=False
    )
```
